512 devices in a mesh: hst: 64 (over y, z_lo, core), head: 8 (over x, z_hi).
Axes of the slice: x: 4, y: 4, z: 16 (z_hi: 2, z_lo: 8; z = z_hi * 8 + z_lo), core: 2. Of those that a mesh axis runs over, the one named last changes fastest.
Arguments:
- queries: bfloat16 [16384, 4096], P('hst', 'head')
- keys: bfloat16 [16384, 1024], P('hst', 'head')
- values: bfloat16 [16384, 1024], P('hst', 'head'), may hold values from -24 to 24
- passing_index: int32 [64, 128], P('hst'), may hold values from 0 to 255, as said below
- out_weight: bfloat16 [4096, 4096], P('head'), may hold values from -0.09375 to 0.09375
Outputs:
- mixed: bfloat16 [16384, 4096], P('hst', 'head')
The draws below stay inside these ranges and needn't reach their ends.
Inputs may be any that keep to these rules, and one draw needn't show every extreme that they name: `passing_index`: each shard's 128 positions are distinct.
All inputs are finite; a program needn't handle non-finite values.
Results may differ from the reference program's by a relative error of at most 0.019.
Values may be sent and summed in bfloat16 or wider, within the bound.
No kernel may reach another device: no remote copies, remote signals or barrier semaphores. Data moves between devices by JAX's collectives and lax.ppermute only.
A program may use at most 64 MiB of HBM per device.

```python
import math
import jax
import jax.numpy as jnp
from jax import lax

D = 4096
QH = 32
KVH = 8
HD = 128
ROWS_DEV = 256
PASS = 128
ANCHOR = 128
SHARDS = 64
TOKENS = 16384


def common_keys(key):
    return jax.random.truncated_normal(key, -4.5, 4.5, (TOKENS, KVH * HD), jnp.float32)


def draw_keys(key, part):
    base = common_keys(key)
    return base.astype(jnp.bfloat16)


def draw_queries(key, part):
    key = jax.random.fold_in(key, 23)
    return jax.random.normal(key, (TOKENS, QH * HD), jnp.float32).astype(jnp.bfloat16)


def draw_passing_index(key, part):
    key = jax.random.fold_in(key, 37)
    shard_keys = jax.random.split(key, SHARDS)
    return jax.vmap(lambda shard_key: jax.random.permutation(shard_key, ROWS_DEV)[:PASS])(shard_keys).astype(jnp.int32)


def block_levels(rng, extent, cuts, low, largest):
    level = 1.0
    for position, blocks in cuts:
        heights = jax.random.uniform(jax.random.fold_in(jax.random.fold_in(rng, 6), position), (blocks,), jnp.float32, low / len(cuts), largest / len(cuts))
        level = level * jnp.repeat(jnp.exp(heights), extent[position] // blocks).reshape((-1,) + (1,) * (len(extent) - 1 - position))
    return level


def scatter_about(key, dims, deviation, most, cuts=(), dtype=jnp.bfloat16):
    values = deviation * jax.random.normal(key, dims, jnp.float32)
    if cuts:
        values = values * block_levels(key, dims, cuts, -0.22, 0.18)
    return jnp.clip(values, -most, most).astype(dtype)


def setup_inputs(seed: int = 0) -> dict:
    key_list = jax.random.split(jax.random.key(seed), 6)
    return {
        "queries": draw_queries(jax.random.fold_in(key_list[5], 71), 0),
        "keys": draw_keys(jax.random.fold_in(key_list[5], 71), 0),
        "values": scatter_about(key_list[2], (TOKENS, KVH * HD), 4.0, 24.0, ((0, 64), (1, 8))),
        "passing_index": draw_passing_index(jax.random.fold_in(key_list[5], 71), 0),
        "out_weight": scatter_about(key_list[4], (QH * HD, D), (QH * HD) ** -0.5, 0.09375, ((0, 8),)),
    }


neg_big = -1e+30

def reference(queries, keys, values, passing_index, out_weight):
    groups = QH // KVH
    query_blocks = queries.reshape(SHARDS, ROWS_DEV, KVH, groups, HD)
    key_blocks = keys.reshape(SHARDS, ROWS_DEV, KVH, HD)
    value_blocks = values.reshape(SHARDS, ROWS_DEV, KVH, HD)
    selected = passing_index.astype(jnp.int32)
    pass_keys = jnp.take_along_axis(key_blocks, selected[:, :, None, None], axis=1).reshape(SHARDS * PASS, KVH, HD)
    pass_values = jnp.take_along_axis(value_blocks, selected[:, :, None, None], axis=1).reshape(SHARDS * PASS, KVH, HD)
    anchor_keys = key_blocks[0, :ANCHOR]
    anchor_values = value_blocks[0, :ANCHOR]
    source_shard = jnp.arange(SHARDS * PASS) // PASS
    positions = jnp.arange(ROWS_DEV)

    def per_shard(shard_index):
        shard_queries = query_blocks[shard_index]
        all_keys = jnp.concatenate((anchor_keys, pass_keys, key_blocks[shard_index]), axis=0)
        all_values = jnp.concatenate((anchor_values, pass_values, value_blocks[shard_index]), axis=0)
        visible = jnp.concatenate((jnp.broadcast_to(shard_index > 0, (ROWS_DEV, ANCHOR)), jnp.broadcast_to((source_shard < shard_index)[None, :], (ROWS_DEV, SHARDS * PASS)), positions[:, None] >= positions[None, :]), axis=1)

        def per_head(head_index):
            head_queries = shard_queries[:, head_index].astype(jnp.float32)
            head_keys = all_keys[:, head_index].astype(jnp.float32)
            head_values = all_values[:, head_index].astype(jnp.float32)
            scores = jnp.einsum('rgd,nd->grn', head_queries, head_keys) / math.sqrt(HD)
            masked = jnp.where(visible[None], scores, neg_big)
            top_score = lax.optimization_barrier(jnp.max(masked, axis=-1, keepdims=True))
            weights = jnp.where(visible[None], jnp.exp(masked - top_score), 0.0)
            row_mass = lax.optimization_barrier(jnp.sum(weights, axis=-1))
            rounded = weights.astype(jnp.bfloat16).astype(jnp.float32)
            result = jnp.einsum('grn,nd->grd', rounded, head_values) / row_mass[..., None]
            return result.astype(jnp.bfloat16)
        heads = lax.map(per_head, jnp.arange(KVH))
        return heads.transpose(2, 0, 1, 3).reshape(ROWS_DEV, QH * HD)
    attended = lax.map(per_shard, jnp.arange(SHARDS)).reshape(SHARDS * ROWS_DEV, QH * HD)
    return jnp.dot(attended, out_weight, preferred_element_type=jnp.float32).astype(jnp.bfloat16)
```

```python
import math

import jax
import jax.numpy as jnp
from jax import lax
from jax.experimental import pallas as pl
from jax.experimental.pallas import tpu as pltpu
from jax.sharding import PartitionSpec as P

HD = 128
PASS = 128
ANCHOR = 128
GROUPS = 4
ROWS = 256
HALF = ROWS // 2
QROWS = ROWS * GROUPS
HROWS = HALF * GROUPS
SCALE = math.log2(math.e) / math.sqrt(HD)
LOW = -1e30
BF = jnp.bfloat16
F32 = jnp.float32
VM = pl.BlockSpec(memory_space=pltpu.VMEM)
SM = pl.BlockSpec(memory_space=pltpu.SMEM)
ANY = pl.BlockSpec(memory_space=pl.ANY)


def params():
    return pltpu.CompilerParams(vmem_limit_bytes=48 * 1024 * 1024)


def dot_nt(a, b):
    return lax.dot_general(a, b, (((1,), (1,)), ((), ())), preferred_element_type=F32)


def prepare(index_ref, key_ref, value_ref, query_ref, passed_ref, anchor_ref, scaled_ref):
    rows = lax.broadcasted_iota(jnp.int32, (ROWS, PASS), 0)
    pick = jnp.where(rows == index_ref[...], 1.0, 0.0).astype(BF)
    both = jnp.concatenate([key_ref[...], value_ref[...]], axis=1)
    passed_ref[...] = lax.dot_general(
        pick, both, (((0,), (0,)), ((), ())), preferred_element_type=F32
    ).astype(BF)
    anchor_ref[...] = both[:ANCHOR]
    for half in range(2):
        for g in range(GROUPS):
            part = query_ref[half * HALF : (half + 1) * HALF, g * HD : (g + 1) * HD].astype(F32) * SCALE
            high = part.astype(BF)
            low = (part - high.astype(F32)).astype(BF)
            start = half * HROWS + g * HALF
            scaled_ref[start : start + HALF, :] = jnp.concatenate([high, low], axis=1)


def attend(scaled, acc_ref, top_ref, blocks, masks=None, first=False):
    scores = []
    for number, block in enumerate(blocks):
        keys = block[:, :HD]
        s = dot_nt(scaled, jnp.concatenate([keys, keys], axis=1))
        if masks is not None:
            s = jnp.where(masks[number], s, LOW)
        scores.append(s)
    high = None
    for s in scores:
        for j in range(s.shape[1] // HD):
            part = s[:, j * HD : (j + 1) * HD]
            high = part if high is None else jnp.maximum(high, part)
    high = jnp.max(high, axis=1, keepdims=True)
    if first:
        new = jnp.broadcast_to(high, (high.shape[0], HD))
    else:
        old = top_ref[...]
        new = jnp.maximum(old, high)
    total = None
    for s, block in zip(scores, blocks):
        weights = jnp.concatenate(
            [jnp.exp2(s[:, j * HD : (j + 1) * HD] - new).astype(BF) for j in range(s.shape[1] // HD)], axis=1
        )
        values = jnp.concatenate([block[:, HD:], jnp.ones((block.shape[0], HD), BF)], axis=1)
        part = jnp.dot(weights, values, preferred_element_type=F32)
        total = part if total is None else total + part
    if not first:
        shrink = jnp.exp2(old - new)
        total = acc_ref[...] * jnp.concatenate([shrink, shrink], axis=1) + total
    acc_ref[...] = total
    top_ref[...] = new


def own_row(flag_ref, scaled_ref, key_ref, value_ref, near_ref, near2_ref, far_ref, far2_ref, acc_ref, top_ref):
    scaled = scaled_ref[...]
    token = lax.broadcasted_iota(jnp.int32, (QROWS, ROWS), 0)
    token = token % HALF + (token // HROWS) * HALF
    key = lax.broadcasted_iota(jnp.int32, (QROWS, ROWS), 1)
    local = jnp.concatenate([key_ref[...], value_ref[...]], axis=1)
    attend(scaled, acc_ref, top_ref, [local], [key <= token], first=True)

    @pl.when(flag_ref[0] != 0)
    def _():
        attend(scaled_ref[...], acc_ref, top_ref, [near2_ref[:PASS]])

    @pl.when(flag_ref[1] != 0)
    def _():
        attend(scaled_ref[...], acc_ref, top_ref, [near_ref[PASS : 2 * PASS], near2_ref[PASS : 2 * PASS]])

    @pl.when(flag_ref[2] != 0)
    def _():
        attend(scaled_ref[...], acc_ref, top_ref, [near_ref[2 * PASS :], near2_ref[2 * PASS :]])

    @pl.when(flag_ref[3] != 0)
    def _():
        attend(scaled_ref[...], acc_ref, top_ref, [far_ref[...], far2_ref[...]])


def other_rows(flag_ref, scaled_ref, acc_in, top_in, ours_ref, theirs_ref, acc_ref, top_ref):
    acc_ref[...] = acc_in[...]
    top_ref[...] = top_in[...]
    size = 4 * PASS
    for j in range(3):

        @pl.when(flag_ref[4 + j] != 0)
        def _():
            attend(
                scaled_ref[...],
                acc_ref,
                top_ref,
                [ours_ref[j * size : (j + 1) * size], theirs_ref[j * size : (j + 1) * size]],
            )

    @pl.when(flag_ref[7] != 0)
    def _():
        attend(scaled_ref[...], acc_ref, top_ref, [ours_ref[3 * size :]])

    @pl.when(flag_ref[8] != 0)
    def _():
        attend(scaled_ref[...], acc_ref, top_ref, [theirs_ref[3 * size :]])


def finish(half, flag_ref, scaled_ref, acc_in, top_in, ours_ref, theirs_ref, *rest):
    if half == 0:
        weight_ref, attended_ref, *outs, acc_ref, top_ref, held, sem = rest
    else:
        before_ref, weight_ref, *outs, acc_ref, top_ref, held, sem = rest
    copy = pltpu.make_async_copy(weight_ref, held, sem)
    copy.start()
    span = slice(half * HROWS, (half + 1) * HROWS)
    acc_ref[...] = acc_in[span]
    top_ref[...] = top_in[span]
    size = 4 * PASS
    for j in range(3):

        @pl.when(flag_ref[4 + j] != 0)
        def _():
            attend(
                scaled_ref[span],
                acc_ref,
                top_ref,
                [ours_ref[j * size : (j + 1) * size], theirs_ref[j * size : (j + 1) * size]],
            )

    result = (acc_ref[:, :HD] / acc_ref[:, HD:]).astype(BF)
    attended = jnp.concatenate([result[g * HALF : (g + 1) * HALF] for g in range(GROUPS)], axis=1)
    copy.wait()
    x, h = flag_ref[9], flag_ref[10]
    width = GROUPS * HD

    def project(rows, step, side):
        start = pl.multiple_of((lax.rem(x + step, 4) * 2 + side) * width, width)
        return jnp.dot(rows, held[:, pl.ds(start, width)], preferred_element_type=F32).astype(BF)

    for step in range(4):
        outs[step][...] = project(attended, step, 1 - h)
    if half == 0:
        attended_ref[...] = attended
    else:
        whole = jnp.concatenate([before_ref[...], attended], axis=0)
        for step in range(4):
            outs[4 + step][...] = project(whole, step, h)


def shape(*dims, dtype=BF):
    return jax.ShapeDtypeStruct(dims, dtype)


def shards(queries, keys, values, passing_index, out_weight):
    me = lax.axis_index("hst")
    head = lax.axis_index("head")
    y, z, c = me // 16, (me // 2) % 8, me % 2

    def over_z(value, k):
        return lax.ppermute(value, "hst", [(i, i ^ (2 * k)) for i in range(64)])

    def over_core(value):
        return lax.ppermute(value, "hst", [(i, i ^ 1) for i in range(64)])

    def over_y(value, pairs):
        return lax.ppermute(value, "hst", [(16 * a + i, 16 * b + i) for a, b in pairs for i in range(16)])

    flags = jnp.stack(
        [
            c,
            z & 1,
            z & 2,
            z & 4,
            y >= 1,
            y == 3,
            y >= 2,
            (me > 0) & (c == 0),
            c == 1,
            head // 2,
            head % 2,
        ]
    ).astype(jnp.int32)

    passed, anchor, scaled = pl.pallas_call(
        prepare,
        out_shape=(shape(PASS, 2 * HD), shape(ANCHOR, 2 * HD), shape(QROWS, 2 * HD)),
        in_specs=[VM] * 4,
        out_specs=(VM,) * 3,
        compiler_params=params(),
    )(passing_index, keys, values, queries)

    mirror = over_z(passed, 4)
    near = jnp.concatenate([passed] + [over_z(passed, k) for k in (1, 2, 3)], axis=0)
    far = jnp.concatenate([mirror] + [over_z(mirror, k) for k in (1, 2, 3)], axis=0)

    anchor = jnp.where(me == 0, anchor, jnp.zeros_like(anchor))
    sources = [0]
    for bit in (16, 48, 8, 4, 2):
        if bit == 48:
            pairs = [(0, 48), (16, 32)]
        else:
            pairs = [(s, s + bit) for s in sources]
        anchor = anchor + lax.ppermute(anchor, "hst", pairs)
        sources = sources + [b for _, b in pairs]

    rounds = (((0, 1), (1, 2), (2, 3)), ((0, 3),), ((0, 2), (1, 3)))
    near_y = jnp.concatenate([over_y(near, pairs) for pairs in rounds] + [anchor], axis=0)
    far_y = jnp.concatenate([over_y(far, pairs) for pairs in rounds], axis=0)

    near2, far2 = over_core(near), over_core(far)
    near_y2, far_y2 = over_core(near_y), over_core(far_y)

    state = (shape(QROWS, 2 * HD, dtype=F32), shape(QROWS, HD, dtype=F32))
    acc, top = pl.pallas_call(
        own_row,
        out_shape=state,
        in_specs=[SM] + [VM] * 7,
        out_specs=(VM,) * 2,
        compiler_params=params(),
    )(flags, scaled, keys, values, near, near2, far, far2)
    acc, top = pl.pallas_call(
        other_rows,
        out_shape=state,
        in_specs=[SM] + [VM] * 5,
        out_specs=(VM,) * 2,
        compiler_params=params(),
    )(flags, scaled, acc, top, near_y, near_y2)

    width = GROUPS * HD
    scratch = [
        pltpu.VMEM((HROWS, 2 * HD), F32),
        pltpu.VMEM((HROWS, HD), F32),
        pltpu.VMEM(out_weight.shape, BF),
        pltpu.SemaphoreType.DMA,
    ]

    def finish_first(*args):
        finish(0, *args)

    def finish_second(*args):
        finish(1, *args)

    attended, *away_a = pl.pallas_call(
        finish_first,
        out_shape=(shape(HALF, width),) * 5,
        in_specs=[SM] + [VM] * 5 + [ANY],
        out_specs=(VM,) * 5,
        scratch_shapes=scratch,
        compiler_params=params(),
    )(flags, scaled, acc, top, far_y, far_y2, out_weight)
    outs = pl.pallas_call(
        finish_second,
        out_shape=(shape(HALF, width),) * 4 + (shape(ROWS, width),) * 4,
        in_specs=[SM] + [VM] * 6 + [ANY],
        out_specs=(VM,) * 8,
        scratch_shapes=scratch,
        compiler_params=params(),
    )(flags, scaled, acc, top, far_y, far_y2, attended, out_weight)
    away_b, home = outs[:4], outs[4:]

    def sum_over_x(parts):
        total = parts[0].astype(F32)
        for step in (1, 2, 3):
            pairs = [(2 * a + s, 2 * ((a + step) % 4) + s) for a in range(4) for s in range(2)]
            total = total + lax.ppermute(parts[step], "head", pairs).astype(F32)
        return total

    def over_h(value):
        return lax.ppermute(value, "head", [(i, i ^ 1) for i in range(8)])

    other_a = over_h(sum_over_x(away_a).astype(BF))
    other_b = over_h(sum_over_x(away_b).astype(BF))
    mine = sum_over_x(home)
    return (mine + jnp.concatenate([other_a, other_b], axis=0).astype(F32)).astype(BF)


def solution(mesh):
    in_specs = (
        P("hst", "head"),
        P("hst", "head"),
        P("hst", "head"),
        P("hst", None),
        P("head", None),
    )
    out_specs = P("hst", "head")
    return jax.shard_map(shards, mesh=mesh, in_specs=in_specs, out_specs=out_specs, check_vma=False)
```

```python
import math

import jax
import jax.numpy as jnp
from jax import lax
from jax.experimental import pallas as pl
from jax.experimental.pallas import tpu as pltpu
from jax.sharding import PartitionSpec as P

HD = 128
PASS = 128
ANCHOR = 128
GROUPS = 4
ROWS = 256
HALF = ROWS // 2
QROWS = ROWS * GROUPS
HROWS = HALF * GROUPS
TILE = 512
SCALE = math.log2(math.e) / math.sqrt(HD)
LOW = -1e30
BF = jnp.bfloat16
F32 = jnp.float32
VM = pl.BlockSpec(memory_space=pltpu.VMEM)
SM = pl.BlockSpec(memory_space=pltpu.SMEM)
ANY = pl.BlockSpec(memory_space=pl.ANY)


def params():
    return pltpu.CompilerParams(vmem_limit_bytes=20 * 2**20)


def dot_nt(a, b):
    return lax.dot_general(a, b, (((1,), (1,)), ((), ())), preferred_element_type=F32)


def prepare(place_ref, index_ref, key_ref, value_ref, query_ref, passed_ref, anchor_ref, scaled_ref):
    rows = lax.broadcasted_iota(jnp.int32, (ROWS, PASS), 0)
    pick = jnp.where(rows == index_ref[...], 1.0, 0.0).astype(BF)
    both = jnp.concatenate([key_ref[...], value_ref[...]], axis=1)
    passed_ref[...] = lax.dot_general(
        pick, both, (((0,), (0,)), ((), ())), preferred_element_type=F32
    ).astype(BF)
    anchor_ref[...] = jnp.where(place_ref[0] == 0, both[:ANCHOR], jnp.zeros_like(both[:ANCHOR]))
    for half in range(2):
        for g in range(GROUPS):
            part = query_ref[half * HALF : (half + 1) * HALF, g * HD : (g + 1) * HD].astype(F32) * SCALE
            high = part.astype(BF)
            low = (part - high.astype(F32)).astype(BF)
            start = half * HROWS + g * HALF
            scaled_ref[start : start + HALF, :] = jnp.concatenate([high, low], axis=1)


def position(place_ref):
    me = place_ref[0]
    return me // 16, lax.rem(me // 2, 8), lax.rem(me, 2)


def tile(scaled_ref, acc_ref, top_ref, start, key, value, mask, first):
    span = slice(start, start + TILE)
    s = dot_nt(scaled_ref[span], key)
    if mask is not None:
        s = jnp.where(mask, s, LOW)
    parts = [s[:, j * HD : (j + 1) * HD] for j in range(s.shape[1] // HD)]
    high = parts[0]
    for part in parts[1:]:
        high = jnp.maximum(high, part)
    high = jnp.max(high, axis=1, keepdims=True)
    if first:
        new = jnp.broadcast_to(high, (TILE, HD))
    else:
        old = top_ref[span]
        new = jnp.maximum(old, high)
    weights = jnp.concatenate([jnp.exp2(part - new).astype(BF) for part in parts], axis=1)
    total = jnp.dot(weights, value, preferred_element_type=F32)
    if not first:
        shrink = jnp.exp2(old - new)
        total = acc_ref[span] * jnp.concatenate([shrink, shrink], axis=1) + total
    acc_ref[span] = total
    top_ref[span] = new


def attend(scaled_ref, acc_ref, top_ref, blocks, masks=None, first=False):
    block = blocks[0] if len(blocks) == 1 else jnp.concatenate(blocks, axis=0)
    keys, count = block[:, :HD], block.shape[0]
    key = jnp.concatenate([keys, keys], axis=1)
    value = jnp.concatenate([block[:, HD:], jnp.ones((count, HD), BF)], axis=1)
    for number in range(QROWS // TILE):
        mask = None if masks is None else masks[number]
        tile(scaled_ref, acc_ref, top_ref, number * TILE, key, value, mask, first)


def own_tokens(scaled_ref, key_ref, value_ref, acc_ref, top_ref):
    token = lax.broadcasted_iota(jnp.int32, (TILE, ROWS), 0) % HALF
    key = lax.broadcasted_iota(jnp.int32, (TILE, ROWS), 1)
    masks = [key <= token + (number * TILE // HROWS) * HALF for number in range(QROWS // TILE)]
    local = jnp.concatenate([key_ref[...], value_ref[...]], axis=1)
    attend(scaled_ref, acc_ref, top_ref, [local], masks, first=True)


def visit(place_ref, scaled_ref, acc_ref, top_ref, pieces, spots):
    y, z, _ = position(place_ref)
    for row in range(3):

        @pl.when(row < y)
        def _():
            for piece in pieces:
                attend(scaled_ref, acc_ref, top_ref, [piece[row, : 4 * PASS]])

    def own_row(bit):
        parts = []
        for spot, k in enumerate(spots):
            if k and bit <= k < 2 * bit:
                parts += [piece[y, spot * PASS : (spot + 1) * PASS] for piece in pieces]
        return parts

    for bit in (1, 2, 4):
        if any(bit <= k < 2 * bit for k in spots):

            @pl.when(lax.rem(z // bit, 2) == 1)
            def _():
                attend(scaled_ref, acc_ref, top_ref, own_row(bit))


def visit_anchor(place_ref, scaled_ref, acc_ref, top_ref, piece, core):
    me = place_ref[0]

    @pl.when((lax.rem(me, 2) == core) & (me > 0))
    def _():
        attend(scaled_ref, acc_ref, top_ref, [piece[0, 4 * PASS :]])


NEAR = (0, 4, 2, 6)
FAR = (1, 5, 3, 7)


def attend_near(place_ref, scaled_ref, acc_in, top_in, ours_ref, theirs_ref, acc_ref, top_ref):
    acc_ref[...] = acc_in[...]
    top_ref[...] = top_in[...]
    visit(place_ref, scaled_ref, acc_ref, top_ref, [ours_ref, theirs_ref], NEAR)
    y, _, c = position(place_ref)

    @pl.when(c == 1)
    def _():
        attend(scaled_ref, acc_ref, top_ref, [theirs_ref[y, :PASS]])


def attend_far(place_ref, scaled_ref, acc_in, top_in, ours_ref, acc_ref, top_ref):
    acc_ref[...] = acc_in[...]
    top_ref[...] = top_in[...]
    visit(place_ref, scaled_ref, acc_ref, top_ref, [ours_ref], FAR)
    visit_anchor(place_ref, scaled_ref, acc_ref, top_ref, ours_ref, 0)


def finish(place_ref, scaled_ref, acc_in, top_in, theirs_ref, weight_ref, away_ref, home_ref, acc_ref, top_ref, held, sem):
    copy = pltpu.make_async_copy(weight_ref, held, sem)
    copy.start()
    acc_ref[...] = acc_in[...]
    top_ref[...] = top_in[...]
    visit(place_ref, scaled_ref, acc_ref, top_ref, [theirs_ref], FAR)
    visit_anchor(place_ref, scaled_ref, acc_ref, top_ref, theirs_ref, 1)
    result = (acc_ref[:, :HD] / acc_ref[:, HD:]).astype(BF)
    attended = jnp.concatenate(
        [
            jnp.concatenate(
                [result[half * HROWS + g * HALF : half * HROWS + (g + 1) * HALF] for g in range(GROUPS)], axis=1
            )
            for half in range(2)
        ],
        axis=0,
    )
    copy.wait()
    h = lax.rem(place_ref[1], 2)
    width = GROUPS * HD
    for out, side in ((away_ref, 1 - h), (home_ref, h)):
        for x in range(4):
            start = pl.multiple_of((2 * x + side) * width, width)
            out[x] = jnp.dot(attended, held[:, pl.ds(start, width)], preferred_element_type=F32).astype(BF)


def shape(*dims, dtype=BF):
    return jax.ShapeDtypeStruct(dims, dtype)


def shards(queries, keys, values, passing_index, out_weight):
    me = lax.axis_index("hst")
    head = lax.axis_index("head")

    def over_z(value, k):
        return lax.ppermute(value, "hst", [(i, i ^ (2 * k)) for i in range(64)])

    def over_core(value):
        return lax.ppermute(value, "hst", [(i, i ^ 1) for i in range(64)])

    def over_y(value):
        return lax.all_to_all(
            jnp.broadcast_to(value[None], (4,) + value.shape),
            "hst",
            0,
            0,
            axis_index_groups=[[16 * row + i for row in range(4)] for i in range(16)],
        )

    place = jnp.stack([me, head]).astype(jnp.int32)

    def call(kernel, out_shape, specs, *args, flops=0, moved=0, scratch=()):
        many = isinstance(out_shape, tuple)
        return pl.pallas_call(
            kernel,
            out_shape=out_shape,
            in_specs=specs,
            out_specs=(VM,) * len(out_shape) if many else VM,
            scratch_shapes=scratch,
            compiler_params=params(),
            cost_estimate=pl.CostEstimate(flops=flops, bytes_accessed=moved, transcendentals=0),
        )(*args)

    def attention(kernel, *pieces, keys):
        return call(
            kernel,
            state,
            [SM] + [VM] * (3 + len(pieces)),
            place,
            scaled,
            acc,
            top,
            *pieces,
            flops=8 * QROWS * keys * HD,
            moved=2**20,
        )

    state = (shape(QROWS, 2 * HD, dtype=F32), shape(QROWS, HD, dtype=F32))
    passed, anchor, scaled = call(
        prepare,
        (shape(PASS, 2 * HD), shape(ANCHOR, 2 * HD), shape(QROWS, 2 * HD)),
        [SM] + [VM] * 4,
        place,
        passing_index,
        keys,
        values,
        queries,
        moved=2**20,
    )

    def spread(value, k):
        step = 2 * k
        return value + lax.ppermute(value, "hst", [(i, i + step) for i in range(0, 16, 2 * step)])

    acc, top = call(own_tokens, state, [VM] * 3, scaled, keys, values, flops=8 * QROWS * ROWS * HD, moved=2**20)
    mirror, anchor, acc, top = lax.optimization_barrier((over_z(passed, 4), spread(anchor, 4), acc, top))
    two = jnp.concatenate([passed, mirror], axis=0)
    pair, anchor = lax.optimization_barrier((over_z(two, 2), spread(anchor, 2)))
    near = jnp.concatenate([two, pair], axis=0)
    far = jnp.concatenate([over_z(near, 1), spread(anchor, 1)], axis=0)

    near_y, far = lax.optimization_barrier((over_y(near), far))
    far_y = over_y(far)
    acc, top = attention(attend_near, near_y, over_core(near_y), keys=3840)
    far_y, acc, top = lax.optimization_barrier((far_y, acc, top))
    acc, top = attention(attend_far, far_y, keys=2048)
    far_y2 = over_core(far_y)

    width = GROUPS * HD
    away, home = call(
        finish,
        (shape(4, ROWS, width), shape(4, ROWS, width)),
        [SM] + [VM] * 4 + [ANY],
        place,
        scaled,
        acc,
        top,
        far_y2,
        out_weight,
        flops=8 * QROWS * 3072 * HD,
        moved=2**23,
        scratch=[
            pltpu.VMEM((QROWS, 2 * HD), F32),
            pltpu.VMEM((QROWS, HD), F32),
            pltpu.VMEM(out_weight.shape, BF),
            pltpu.SemaphoreType.DMA,
        ],
    )

    def sum_over_x(parts):
        rows = lax.all_to_all(
            parts, "head", 0, 0, axis_index_groups=[[0, 2, 4, 6], [1, 3, 5, 7]], tiled=True
        )
        return jnp.sum(rows.astype(F32), axis=0)

    other = lax.ppermute(sum_over_x(away).astype(BF), "head", [(i, i ^ 1) for i in range(8)])
    return (sum_over_x(home) + other.astype(F32)).astype(BF)


def solution(mesh):
    in_specs = (
        P("hst", "head"),
        P("hst", "head"),
        P("hst", "head"),
        P("hst", None),
        P("head", None),
    )
    out_specs = P("hst", "head")
    return jax.shard_map(shards, mesh=mesh, in_specs=in_specs, out_specs=out_specs, check_vma=False)
```

```python
import math

import jax
import jax.numpy as jnp
from jax import lax
from jax.experimental import pallas as pl
from jax.experimental.pallas import tpu as pltpu
from jax.sharding import PartitionSpec as P

HD = 128
PASS = 128
ANCHOR = 128
GROUPS = 4
ROWS = 256
HALF = ROWS // 2
QROWS = ROWS * GROUPS
HROWS = HALF * GROUPS
TILE = 512
SCALE = math.log2(math.e) / math.sqrt(HD)
LOW = -1e30
BF = jnp.bfloat16
F32 = jnp.float32
VM = pl.BlockSpec(memory_space=pltpu.VMEM)
SM = pl.BlockSpec(memory_space=pltpu.SMEM)
HBM = pl.BlockSpec(memory_space=pltpu.HBM)


def dot_nt(a, b):
    return lax.dot_general(a, b, (((1,), (1,)), ((), ())), preferred_element_type=F32)


def fetch(pairs, sems):
    copies = [pltpu.make_async_copy(a, b, sems.at[i]) for i, (a, b) in enumerate(pairs)]
    for copy in copies:
        copy.start()
    return copies


def wait(copies):
    for copy in copies:
        copy.wait()


def prepare(place_ref, index_hbm, key_hbm, value_hbm, passed_ref, anchor_ref, index_ref, both_ref, sems):
    wait(
        fetch(
            [(index_hbm, index_ref), (key_hbm, both_ref.at[:, :HD]), (value_hbm, both_ref.at[:, HD:])],
            sems,
        )
    )
    rows = lax.broadcasted_iota(jnp.int32, (ROWS, PASS), 0)
    pick = jnp.where(rows == index_ref[...], 1.0, 0.0).astype(BF)
    both = both_ref[...]
    passed_ref[...] = lax.dot_general(
        pick, both, (((0,), (0,)), ((), ())), preferred_element_type=F32
    ).astype(BF)
    anchor_ref[...] = jnp.where(place_ref[0] == 0, both[:ANCHOR], jnp.zeros_like(both[:ANCHOR]))


def split_weights(place_ref, weight_hbm, *rest):
    *outs, sems = rest
    width = outs[0].shape[1]
    x = place_ref[1] // 2
    pairs = []
    for step, out in enumerate(outs, 1):
        start = pl.multiple_of(lax.rem(x + step, 4) * width, width)
        pairs.append((weight_hbm.at[:, pl.ds(start, width)], out))
    wait(fetch(pairs, sems))


def pack_far(pieces_hbm, anchor_hbm, out_hbm, sems):
    size = pieces_hbm.shape[0]
    copies = fetch([(pieces_hbm, out_hbm.at[y, pl.ds(0, size)]) for y in range(4)], sems)
    wait(copies)
    wait(fetch([(anchor_hbm, out_hbm.at[y, pl.ds(size, PASS)]) for y in range(4)], sems))


def position(place_ref):
    me = place_ref[0]
    return me // 16, lax.rem(me // 2, 8), lax.rem(me, 2)


def tile(scaled_ref, acc_ref, top_ref, start, key, value, mask, first):
    span = slice(start, start + TILE)
    s = dot_nt(scaled_ref[span], key)
    if mask is not None:
        s = jnp.where(mask, s, LOW)
    parts = [s[:, j * HD : (j + 1) * HD] for j in range(s.shape[1] // HD)]
    high = parts[0]
    for part in parts[1:]:
        high = jnp.maximum(high, part)
    high = jnp.max(high, axis=1, keepdims=True)
    if first:
        new = jnp.broadcast_to(high, (TILE, HD))
    else:
        old = top_ref[span]
        new = jnp.maximum(old, high)
    weights = jnp.concatenate([jnp.exp2(part - new).astype(BF) for part in parts], axis=1)
    total = jnp.dot(weights, value, preferred_element_type=F32)
    if not first:
        shrink = jnp.exp2(old - new)
        total = acc_ref[span] * jnp.concatenate([shrink, shrink], axis=1) + total
    acc_ref[span] = total
    top_ref[span] = new


def attend(scaled_ref, acc_ref, top_ref, block, mask=None, first=False):
    keys, count = block[:, :HD], block.shape[0]
    key = jnp.concatenate([keys, keys], axis=1)
    value = jnp.concatenate([block[:, HD:], jnp.ones((count, HD), BF)], axis=1)
    for number in range(QROWS // TILE):
        one = mask(number) if mask is not None else None
        tile(scaled_ref, acc_ref, top_ref, number * TILE, key, value, one, first)


def own_tokens(query_ref, local_ref, scaled_ref, acc_ref, top_ref):
    for half in range(2):
        for g in range(GROUPS):
            part = query_ref[half * HALF : (half + 1) * HALF, g * HD : (g + 1) * HD].astype(F32) * SCALE
            high = part.astype(BF)
            low = (part - high.astype(F32)).astype(BF)
            start = half * HROWS + g * HALF
            scaled_ref[start : start + HALF, :] = jnp.concatenate([high, low], axis=1)
    token = lax.broadcasted_iota(jnp.int32, (TILE, ROWS), 0) % HALF
    key = lax.broadcasted_iota(jnp.int32, (TILE, ROWS), 1)

    def causal(number):
        return key <= token + (number * TILE // HROWS) * HALF

    attend(scaled_ref, acc_ref, top_ref, local_ref[...], causal, first=True)


NEAR = (0, 4, 2, 6)
FAR = (1, 5, 3, 7)


def visit(place_ref, scaled_ref, acc_ref, top_ref, piece, spots, core, anchor):
    y, z, c = position(place_ref)
    me = place_ref[0]
    count = len(spots) * PASS

    def own(anchored):
        def mask(number):
            width = count + (PASS if anchored else 0)
            lane = lax.broadcasted_iota(jnp.int32, (1, width), 1) // PASS
            seen = jnp.zeros((1, width), jnp.bool_)
            for spot, k in enumerate(spots):
                before = (z // (1 << (k.bit_length() - 1))) % 2 == 1 if k else (core < c)
                seen = seen | ((lane == spot) & before)
            if anchored:
                seen = seen | ((lane == len(spots)) & (me > 0) & (core == 0))
            return seen

        return mask

    def anchor_only(number):
        lane = lax.broadcasted_iota(jnp.int32, (1, count + PASS), 1)
        return (lane < count) | (core == 0)

    for row in range(4):
        whole = anchor and row == 0
        width = count + (PASS if whole else 0)

        @pl.when(row < y)
        def _():
            attend(scaled_ref, acc_ref, top_ref, piece[row, :width], anchor_only if whole else None)

        @pl.when(row == y)
        def _():
            attend(scaled_ref, acc_ref, top_ref, piece[row, :width], own(whole))


def attend_near(
    place_ref, query_hbm, key_hbm, value_hbm, ours_hbm, theirs_hbm, scaled_hbm, acc_hbm, top_hbm,
    query_ref, local_ref, ours_ref, theirs_ref, scaled_ref, acc_ref, top_ref, sems,
):
    copies = fetch(
        [
            (query_hbm, query_ref),
            (key_hbm, local_ref.at[:, :HD]),
            (value_hbm, local_ref.at[:, HD:]),
            (ours_hbm, ours_ref),
            (theirs_hbm, theirs_ref),
        ],
        sems,
    )
    wait(copies[:3])
    own_tokens(query_ref, local_ref, scaled_ref, acc_ref, top_ref)
    c = lax.rem(place_ref[0], 2)
    wait(copies[3:4])
    visit(place_ref, scaled_ref, acc_ref, top_ref, ours_ref, NEAR, c, False)
    wait(copies[4:])
    visit(place_ref, scaled_ref, acc_ref, top_ref, theirs_ref, NEAR, 1 - c, False)
    wait(fetch([(scaled_ref, scaled_hbm), (acc_ref, acc_hbm), (top_ref, top_hbm)], sems))


def attend_far(
    place_ref, scaled_hbm, acc_hbm, top_hbm, ours_hbm, theirs_hbm, attended_hbm,
    attended_ref, ours_ref, theirs_ref, scaled_ref, acc_ref, top_ref, sems,
):
    copies = fetch(
        [
            (scaled_hbm, scaled_ref),
            (acc_hbm, acc_ref),
            (top_hbm, top_ref),
            (ours_hbm, ours_ref),
            (theirs_hbm, theirs_ref),
        ],
        sems,
    )
    c = lax.rem(place_ref[0], 2)
    wait(copies[:4])
    visit(place_ref, scaled_ref, acc_ref, top_ref, ours_ref, FAR, c, True)
    wait(copies[4:])
    visit(place_ref, scaled_ref, acc_ref, top_ref, theirs_ref, FAR, 1 - c, True)
    result = (acc_ref[:, :HD] / acc_ref[:, HD:]).astype(BF)
    for half in range(2):
        for g in range(GROUPS):
            start = half * HROWS + g * HALF
            attended_ref[half * HALF : (half + 1) * HALF, g * HD : (g + 1) * HD] = result[start : start + HALF]
    wait(fetch([(attended_ref, attended_hbm.at[x]) for x in range(4)], sems))


def project(away, place_ref, rows_hbm, own_hbm, *rest):
    *sent, out_ref, rows_ref, weight_ref, sems = rest
    x, h = place_ref[1] // 2, lax.rem(place_ref[1], 2)
    side = 1 - h if away else h
    width = out_ref.shape[1]
    pairs = []
    for step in range(4):
        if step:
            start, weight_hbm = side * width, sent[step - 1]
        else:
            start, weight_hbm = (2 * x + side) * width, own_hbm
        columns = pl.ds(pl.multiple_of(start, width), width)
        pairs.append((weight_hbm.at[:, columns], weight_ref.at[step]))
    copies = fetch([(rows_hbm, rows_ref)] + pairs, sems)
    wait(copies)
    total = None
    for step in range(4):
        rows = rows_ref[lax.rem(x + 4 - step, 4)]
        part = jnp.dot(rows, weight_ref[step], preferred_element_type=F32)
        total = part if total is None else total + part
    out_ref[...] = total.astype(out_ref.dtype)


def shape(*dims, dtype=BF):
    return jax.ShapeDtypeStruct(dims, dtype)


def shards(queries, keys, values, passing_index, out_weight):
    me = lax.axis_index("hst")
    head = lax.axis_index("head")

    def over_z(value, k):
        return lax.ppermute(value, "hst", [(i, i ^ (2 * k)) for i in range(64)])

    def over_core(value):
        return lax.ppermute(value, "hst", [(i, i ^ 1) for i in range(64)])

    def four(value):
        return jnp.broadcast_to(value[None], (4,) + value.shape)

    def over_y(value):
        groups = [[16 * row + i for row in range(4)] for i in range(16)]
        return lax.all_to_all(value, "hst", 0, 0, axis_index_groups=groups)

    place = jnp.stack([me, head]).astype(jnp.int32)

    def call(kernel, out_shape, in_specs, out_specs, *args, scratch=(), limit=62 * 2**20, flops=2**20):
        return pl.pallas_call(
            kernel,
            out_shape=out_shape,
            in_specs=in_specs,
            out_specs=out_specs,
            scratch_shapes=scratch,
            compiler_params=pltpu.CompilerParams(vmem_limit_bytes=limit),
            cost_estimate=pl.CostEstimate(flops=flops, bytes_accessed=2**16, transcendentals=0),
        )(*args)

    def spread(value, k):
        step = 2 * k
        return value + lax.ppermute(value, "hst", [(i, i + step) for i in range(0, 16, 2 * step)])

    def over_x(value):
        return lax.all_to_all(value, "head", 0, 0, axis_index_groups=[[0, 2, 4, 6], [1, 3, 5, 7]])

    copies = pltpu.SemaphoreType.DMA((5,))
    passed, anchor = call(
        prepare,
        (shape(PASS, 2 * HD), shape(ANCHOR, 2 * HD)),
        [SM] + [HBM] * 3,
        (VM,) * 2,
        place,
        passing_index,
        keys,
        values,
        scratch=[pltpu.VMEM((1, PASS), jnp.int32), pltpu.VMEM((ROWS, 2 * HD), BF), copies],
    )

    mirror, anchor = over_z(passed, 4), spread(anchor, 4)

    anchor, out_weight = lax.optimization_barrier((anchor, out_weight))
    columns = call(
        split_weights,
        (shape(out_weight.shape[0], out_weight.shape[1] // 4),) * 3,
        [SM, HBM],
        (HBM,) * 3,
        place,
        out_weight,
        scratch=[copies],
    )
    weights = [out_weight]
    for step, value in enumerate(columns, 1):
        pairs = [(2 * a + s, 2 * ((a + step) % 4) + s) for a in range(4) for s in range(2)]
        weights.append(lax.ppermute(value, "head", pairs))

    mirror, anchor = lax.optimization_barrier((mirror, anchor))
    two = jnp.concatenate([passed, mirror], axis=0)
    pair, anchor = lax.optimization_barrier((over_z(two, 2), spread(anchor, 2)))
    near = jnp.concatenate([two, pair], axis=0)
    far = call(
        pack_far,
        shape(4, 5 * PASS, 2 * HD),
        [HBM] * 2,
        HBM,
        over_z(near, 1),
        spread(anchor, 1),
        scratch=[copies],
        flops=2 * 10**9,
    )

    near_y, far, weights[1], weights[3] = lax.optimization_barrier((over_y(four(near)), far, weights[1], weights[3]))
    far_y = over_y(far)
    width = GROUPS * HD
    state = [
        pltpu.VMEM((QROWS, 2 * HD), BF),
        pltpu.VMEM((QROWS, 2 * HD), F32),
        pltpu.VMEM((QROWS, HD), F32),
        copies,
    ]
    scaled, acc, top = call(
        attend_near,
        (shape(QROWS, 2 * HD), shape(QROWS, 2 * HD, dtype=F32), shape(QROWS, HD, dtype=F32)),
        [SM] + [HBM] * 5,
        (HBM,) * 3,
        place,
        queries,
        keys,
        values,
        near_y,
        over_core(near_y),
        scratch=[pltpu.VMEM((ROWS, width), BF), pltpu.VMEM((ROWS, 2 * HD), BF)]
        + [pltpu.VMEM(near_y.shape, BF)] * 2
        + state,
    )
    far_y, acc, top, weights[2] = lax.optimization_barrier((far_y, acc, top, weights[2]))
    attended = call(
        attend_far,
        shape(4, ROWS, width),
        [SM] + [HBM] * 5,
        HBM,
        place,
        scaled,
        acc,
        top,
        far_y,
        over_core(far_y),
        scratch=[pltpu.VMEM((ROWS, width), BF)] + [pltpu.VMEM(far_y.shape, BF)] * 2 + state,
    )

    rows = over_x(attended)

    def side(away):
        def kernel(*refs):
            project(away, *refs)

        return call(
            kernel,
            shape(ROWS, width, dtype=BF if away else F32),
            [SM] + [HBM] * 5,
            VM,
            place,
            rows,
            *weights,
            scratch=[pltpu.VMEM(rows.shape, BF), pltpu.VMEM(rows.shape[:1] + (width, width), BF), copies],
        )

    other = lax.ppermute(side(True), "head", [(i, i ^ 1) for i in range(8)])
    return (side(False) + other.astype(F32)).astype(BF)


def solution(mesh):
    in_specs = (
        P("hst", "head"),
        P("hst", "head"),
        P("hst", "head"),
        P("hst", None),
        P("head", None),
    )
    out_specs = P("hst", "head")
    return jax.shard_map(shards, mesh=mesh, in_specs=in_specs, out_specs=out_specs, check_vma=False)
```

```python
import math

import jax
import jax.numpy as jnp
from jax import lax
from jax.experimental import pallas as pl
from jax.experimental.pallas import tpu as pltpu
from jax.sharding import PartitionSpec as P

HD = 128
PASS = 128
ANCHOR = 128
GROUPS = 4
ROWS = 256
HALF = ROWS // 2
QROWS = ROWS * GROUPS
HROWS = HALF * GROUPS
TILE = 512
SCALE = math.log2(math.e) / math.sqrt(HD)
LOW = -1e30
BF = jnp.bfloat16
F32 = jnp.float32
VM = pl.BlockSpec(memory_space=pltpu.VMEM)
SM = pl.BlockSpec(memory_space=pltpu.SMEM)
HBM = pl.BlockSpec(memory_space=pltpu.HBM)


def dot_nt(a, b):
    return lax.dot_general(a, b, (((1,), (1,)), ((), ())), preferred_element_type=F32)


def fetch(pairs, sems):
    copies = [pltpu.make_async_copy(a, b, sems.at[i]) for i, (a, b) in enumerate(pairs)]
    for copy in copies:
        copy.start()
    return copies


def wait(copies):
    for copy in copies:
        copy.wait()


def prepare(place_ref, index_hbm, key_hbm, value_hbm, passed_ref, anchor_ref, index_ref, both_ref, sems):
    wait(
        fetch(
            [(index_hbm, index_ref), (key_hbm, both_ref.at[:, :HD]), (value_hbm, both_ref.at[:, HD:])],
            sems,
        )
    )
    rows = lax.broadcasted_iota(jnp.int32, (ROWS, PASS), 0)
    pick = jnp.where(rows == index_ref[...], 1.0, 0.0).astype(BF)
    both = both_ref[...]
    passed_ref[...] = lax.dot_general(
        pick, both, (((0,), (0,)), ((), ())), preferred_element_type=F32
    ).astype(BF)
    anchor_ref[...] = jnp.where(place_ref[0] == 0, both[:ANCHOR], jnp.zeros_like(both[:ANCHOR]))


def split_weights(place_ref, weight_hbm, *rest):
    *outs, held_ref, sems = rest
    width = outs[0].shape[1]
    x = place_ref[1] // 2
    pairs = []
    for step in range(1, 4):
        start = pl.multiple_of(lax.rem(x + step, 4) * width, width)
        pairs.append((weight_hbm.at[:, pl.ds(start, width)], held_ref.at[step - 1]))
    wait(fetch(pairs, sems))
    wait(fetch([(held_ref.at[i], out) for i, out in enumerate(outs)], sems))


def pack_far(pieces_hbm, anchor_hbm, out_hbm, held_ref, sems):
    size = pieces_hbm.shape[0]
    wait(fetch([(pieces_hbm, held_ref.at[:size]), (anchor_hbm, held_ref.at[size:])], sems))
    wait(fetch([(held_ref, out_hbm.at[y]) for y in range(4)], sems))


def position(place_ref):
    me = place_ref[0]
    return me // 16, lax.rem(me // 2, 8), lax.rem(me, 2)


def tile(scaled_ref, acc_ref, top_ref, start, key, value, mask, first):
    span = slice(start, start + TILE)
    s = dot_nt(scaled_ref[span], key)
    if mask is not None:
        s = jnp.where(mask, s, LOW)
    parts = [s[:, j * HD : (j + 1) * HD] for j in range(s.shape[1] // HD)]
    high = parts[0]
    for part in parts[1:]:
        high = jnp.maximum(high, part)
    high = jnp.max(high, axis=1, keepdims=True)
    if first:
        new = jnp.broadcast_to(high, (TILE, HD))
    else:
        old = top_ref[span]
        new = jnp.maximum(old, high)
    weights = jnp.concatenate([jnp.exp2(part - new).astype(BF) for part in parts], axis=1)
    total = jnp.dot(weights, value, preferred_element_type=F32)
    if not first:
        shrink = jnp.exp2(old - new)
        total = acc_ref[span] * jnp.concatenate([shrink, shrink], axis=1) + total
    acc_ref[span] = total
    top_ref[span] = new


def attend(scaled_ref, acc_ref, top_ref, block, mask=None, first=False):
    keys, count = block[:, :HD], block.shape[0]
    key = jnp.concatenate([keys, keys], axis=1)
    value = jnp.concatenate([block[:, HD:], jnp.ones((count, HD), BF)], axis=1)
    for number in range(QROWS // TILE):
        one = mask(number) if mask is not None else None
        tile(scaled_ref, acc_ref, top_ref, number * TILE, key, value, one, first)


def own_tokens(query_ref, local_ref, scaled_ref, acc_ref, top_ref):
    for half in range(2):
        for g in range(GROUPS):
            part = query_ref[half * HALF : (half + 1) * HALF, g * HD : (g + 1) * HD].astype(F32) * SCALE
            high = part.astype(BF)
            low = (part - high.astype(F32)).astype(BF)
            start = half * HROWS + g * HALF
            scaled_ref[start : start + HALF, :] = jnp.concatenate([high, low], axis=1)
    token = lax.broadcasted_iota(jnp.int32, (TILE, ROWS), 0) % HALF
    key = lax.broadcasted_iota(jnp.int32, (TILE, ROWS), 1)

    def causal(number):
        return key <= token + (number * TILE // HROWS) * HALF

    attend(scaled_ref, acc_ref, top_ref, local_ref[...], causal, first=True)


NEAR = (0, 4, 2, 6)
FAR = (1, 5, 3, 7)


def visit(place_ref, scaled_ref, acc_ref, top_ref, piece, spots, core, anchor):
    y, z, c = position(place_ref)
    me = place_ref[0]
    count = len(spots) * PASS

    def own(anchored):
        def mask(number):
            width = count + (PASS if anchored else 0)
            lane = lax.broadcasted_iota(jnp.int32, (1, width), 1) // PASS
            seen = jnp.zeros((1, width), jnp.bool_)
            for spot, k in enumerate(spots):
                before = (z // (1 << (k.bit_length() - 1))) % 2 == 1 if k else (core < c)
                seen = seen | ((lane == spot) & before)
            if anchored:
                seen = seen | ((lane == len(spots)) & (me > 0) & (core == 0))
            return seen

        return mask

    def anchor_only(number):
        lane = lax.broadcasted_iota(jnp.int32, (1, count + PASS), 1)
        return (lane < count) | (core == 0)

    for row in range(4):
        whole = anchor and row == 0
        width = count + (PASS if whole else 0)

        @pl.when(row < y)
        def _():
            attend(scaled_ref, acc_ref, top_ref, piece[row, :width], anchor_only if whole else None)

        @pl.when(row == y)
        def _():
            attend(scaled_ref, acc_ref, top_ref, piece[row, :width], own(whole))


def attend_near(
    place_ref, query_hbm, key_hbm, value_hbm, ours_hbm, theirs_hbm, scaled_hbm, acc_hbm, top_hbm,
    query_ref, local_ref, ours_ref, theirs_ref, scaled_ref, acc_ref, top_ref, sems,
):
    copies = fetch(
        [
            (query_hbm, query_ref),
            (key_hbm, local_ref.at[:, :HD]),
            (value_hbm, local_ref.at[:, HD:]),
            (ours_hbm, ours_ref),
            (theirs_hbm, theirs_ref),
        ],
        sems,
    )
    wait(copies[:3])
    own_tokens(query_ref, local_ref, scaled_ref, acc_ref, top_ref)
    c = lax.rem(place_ref[0], 2)
    wait(copies[3:4])
    visit(place_ref, scaled_ref, acc_ref, top_ref, ours_ref, NEAR, c, False)
    wait(copies[4:])
    visit(place_ref, scaled_ref, acc_ref, top_ref, theirs_ref, NEAR, 1 - c, False)
    wait(fetch([(scaled_ref, scaled_hbm), (acc_ref, acc_hbm), (top_ref, top_hbm)], sems))


def attend_far(
    place_ref, scaled_hbm, acc_hbm, top_hbm, ours_hbm, theirs_hbm, attended_hbm,
    attended_ref, ours_ref, theirs_ref, scaled_ref, acc_ref, top_ref, sems,
):
    copies = fetch(
        [
            (scaled_hbm, scaled_ref),
            (acc_hbm, acc_ref),
            (top_hbm, top_ref),
            (ours_hbm, ours_ref),
            (theirs_hbm, theirs_ref),
        ],
        sems,
    )
    c = lax.rem(place_ref[0], 2)
    wait(copies[:4])
    visit(place_ref, scaled_ref, acc_ref, top_ref, ours_ref, FAR, c, True)
    wait(copies[4:])
    visit(place_ref, scaled_ref, acc_ref, top_ref, theirs_ref, FAR, 1 - c, True)
    result = (acc_ref[:, :HD] / acc_ref[:, HD:]).astype(BF)
    for half in range(2):
        for g in range(GROUPS):
            start = half * HROWS + g * HALF
            attended_ref[half * HALF : (half + 1) * HALF, g * HD : (g + 1) * HD] = result[start : start + HALF]
    wait(fetch([(attended_ref, attended_hbm.at[x]) for x in range(4)], sems))


def project(away, place_ref, rows_hbm, own_hbm, *rest):
    *sent, out_ref, rows_ref, weight_ref, sems = rest
    x, h = place_ref[1] // 2, lax.rem(place_ref[1], 2)
    side = 1 - h if away else h
    width = out_ref.shape[1]
    pairs = []
    for step in range(4):
        if step:
            start, weight_hbm = side * width, sent[step - 1]
        else:
            start, weight_hbm = (2 * x + side) * width, own_hbm
        columns = pl.ds(pl.multiple_of(start, width), width)
        pairs.append((weight_hbm.at[:, columns], weight_ref.at[step]))
    copies = fetch([(rows_hbm, rows_ref)] + pairs, sems)
    wait(copies)
    total = None
    for step in range(4):
        rows = rows_ref[lax.rem(x + 4 - step, 4)]
        part = jnp.dot(rows, weight_ref[step], preferred_element_type=F32)
        total = part if total is None else total + part
    out_ref[...] = total.astype(out_ref.dtype)


def shape(*dims, dtype=BF):
    return jax.ShapeDtypeStruct(dims, dtype)


def shards(queries, keys, values, passing_index, out_weight):
    me = lax.axis_index("hst")
    head = lax.axis_index("head")

    def over_z(value, k):
        return lax.ppermute(value, "hst", [(i, i ^ (2 * k)) for i in range(64)])

    def over_core(value):
        return lax.ppermute(value, "hst", [(i, i ^ 1) for i in range(64)])

    def four(value):
        return jnp.broadcast_to(value[None], (4,) + value.shape)

    def over_y(value):
        groups = [[16 * row + i for row in range(4)] for i in range(16)]
        return lax.all_to_all(value, "hst", 0, 0, axis_index_groups=groups)

    place = jnp.stack([me, head]).astype(jnp.int32)

    def call(kernel, out_shape, in_specs, out_specs, *args, scratch=(), limit=62 * 2**20, flops=2**20):
        return pl.pallas_call(
            kernel,
            out_shape=out_shape,
            in_specs=in_specs,
            out_specs=out_specs,
            scratch_shapes=scratch,
            compiler_params=pltpu.CompilerParams(vmem_limit_bytes=limit),
            cost_estimate=pl.CostEstimate(flops=flops, bytes_accessed=2**16, transcendentals=0),
        )(*args)

    def spread(value, k):
        step = 2 * k
        return value + lax.ppermute(value, "hst", [(i, i + step) for i in range(0, 16, 2 * step)])

    def over_x(value):
        return lax.all_to_all(value, "head", 0, 0, axis_index_groups=[[0, 2, 4, 6], [1, 3, 5, 7]])

    copies = pltpu.SemaphoreType.DMA((5,))
    passed, anchor = call(
        prepare,
        (shape(PASS, 2 * HD), shape(ANCHOR, 2 * HD)),
        [SM] + [HBM] * 3,
        (VM,) * 2,
        place,
        passing_index,
        keys,
        values,
        scratch=[pltpu.VMEM((1, PASS), jnp.int32), pltpu.VMEM((ROWS, 2 * HD), BF), copies],
    )

    mirror, anchor = over_z(passed, 4), spread(anchor, 4)

    anchor, out_weight = lax.optimization_barrier((anchor, out_weight))
    columns = call(
        split_weights,
        (shape(out_weight.shape[0], out_weight.shape[1] // 4),) * 3,
        [SM, HBM],
        (HBM,) * 3,
        place,
        out_weight,
        scratch=[pltpu.VMEM((3, out_weight.shape[0], out_weight.shape[1] // 4), BF), copies],
    )
    weights = [out_weight]
    for step, value in enumerate(columns, 1):
        pairs = [(2 * a + s, 2 * ((a + step) % 4) + s) for a in range(4) for s in range(2)]
        weights.append(lax.ppermute(value, "head", pairs))

    mirror, anchor = lax.optimization_barrier((mirror, anchor))
    two = jnp.concatenate([passed, mirror], axis=0)
    pair, anchor = lax.optimization_barrier((over_z(two, 2), spread(anchor, 2)))
    near = jnp.concatenate([two, pair], axis=0)
    far = call(
        pack_far,
        shape(4, 5 * PASS, 2 * HD),
        [HBM] * 2,
        HBM,
        over_z(near, 1),
        spread(anchor, 1),
        scratch=[pltpu.VMEM((5 * PASS, 2 * HD), BF), copies],
        flops=2 * 10**9,
    )

    near_y, far, weights[1], weights[3] = lax.optimization_barrier((over_y(four(near)), far, weights[1], weights[3]))
    far_y = over_y(far)
    width = GROUPS * HD
    state = [
        pltpu.VMEM((QROWS, 2 * HD), BF),
        pltpu.VMEM((QROWS, 2 * HD), F32),
        pltpu.VMEM((QROWS, HD), F32),
        copies,
    ]
    scaled, acc, top = call(
        attend_near,
        (shape(QROWS, 2 * HD), shape(QROWS, 2 * HD, dtype=F32), shape(QROWS, HD, dtype=F32)),
        [SM] + [HBM] * 5,
        (HBM,) * 3,
        place,
        queries,
        keys,
        values,
        near_y,
        over_core(near_y),
        scratch=[pltpu.VMEM((ROWS, width), BF), pltpu.VMEM((ROWS, 2 * HD), BF)]
        + [pltpu.VMEM(near_y.shape, BF)] * 2
        + state,
    )
    far_y, acc, top, weights[2] = lax.optimization_barrier((far_y, acc, top, weights[2]))
    attended = call(
        attend_far,
        shape(4, ROWS, width),
        [SM] + [HBM] * 5,
        HBM,
        place,
        scaled,
        acc,
        top,
        far_y,
        over_core(far_y),
        scratch=[pltpu.VMEM((ROWS, width), BF)] + [pltpu.VMEM(far_y.shape, BF)] * 2 + state,
    )

    rows = over_x(attended)

    def side(away):
        def kernel(*refs):
            project(away, *refs)

        return call(
            kernel,
            shape(ROWS, width, dtype=BF if away else F32),
            [SM] + [HBM] * 5,
            VM,
            place,
            rows,
            *weights,
            scratch=[pltpu.VMEM(rows.shape, BF), pltpu.VMEM(rows.shape[:1] + (width, width), BF), copies],
        )

    other = lax.ppermute(side(True), "head", [(i, i ^ 1) for i in range(8)])
    return (side(False) + other.astype(F32)).astype(BF)


def solution(mesh):
    in_specs = (
        P("hst", "head"),
        P("hst", "head"),
        P("hst", "head"),
        P("hst", None),
        P("head", None),
    )
    out_specs = P("hst", "head")
    return jax.shard_map(shards, mesh=mesh, in_specs=in_specs, out_specs=out_specs, check_vma=False)
```

```python
import math

import jax
import jax.numpy as jnp
from jax import lax
from jax.experimental import pallas as pl
from jax.experimental.pallas import tpu as pltpu
from jax.sharding import PartitionSpec as P

HD = 128
PASS = 128
ANCHOR = 128
GROUPS = 4
ROWS = 256
HALF = ROWS // 2
QROWS = ROWS * GROUPS
HROWS = HALF * GROUPS
TILE = 512
SCALE = math.log2(math.e) / math.sqrt(HD)
LOW = -1e30
BF = jnp.bfloat16
F32 = jnp.float32
VM = pl.BlockSpec(memory_space=pltpu.VMEM)
SM = pl.BlockSpec(memory_space=pltpu.SMEM)
HBM = pl.BlockSpec(memory_space=pltpu.HBM)


def dot_nt(a, b):
    return lax.dot_general(a, b, (((1,), (1,)), ((), ())), preferred_element_type=F32)


def fetch(pairs, sems):
    copies = [pltpu.make_async_copy(a, b, sems.at[i]) for i, (a, b) in enumerate(pairs)]
    for copy in copies:
        copy.start()
    return copies


def wait(copies):
    for copy in copies:
        copy.wait()


def prepare(place_ref, index_hbm, key_hbm, value_hbm, passed_ref, anchor_ref, index_ref, both_ref, sems):
    wait(
        fetch(
            [(index_hbm, index_ref), (key_hbm, both_ref.at[:, :HD]), (value_hbm, both_ref.at[:, HD:])],
            sems,
        )
    )
    rows = lax.broadcasted_iota(jnp.int32, (ROWS, PASS), 0)
    pick = jnp.where(rows == index_ref[...], 1.0, 0.0).astype(BF)
    both = both_ref[...]
    passed_ref[...] = lax.dot_general(
        pick, both, (((0,), (0,)), ((), ())), preferred_element_type=F32
    ).astype(BF)
    anchor_ref[...] = jnp.where(place_ref[0] == 0, both[:ANCHOR], jnp.zeros_like(both[:ANCHOR]))


def pack_far(pieces_hbm, anchor_hbm, out_hbm, held_ref, sems):
    size = pieces_hbm.shape[0]
    wait(fetch([(pieces_hbm, held_ref.at[:size]), (anchor_hbm, held_ref.at[size:])], sems))
    wait(fetch([(held_ref, out_hbm.at[y]) for y in range(4)], sems))


def position(place_ref):
    me = place_ref[0]
    return me // 16, lax.rem(me // 2, 8), lax.rem(me, 2)


def tile(scaled_ref, acc_ref, top_ref, start, key, value, mask, first):
    span = slice(start, start + TILE)
    s = dot_nt(scaled_ref[span], key)
    if mask is not None:
        s = jnp.where(mask, s, LOW)
    parts = [s[:, j * HD : (j + 1) * HD] for j in range(s.shape[1] // HD)]
    high = parts[0]
    for part in parts[1:]:
        high = jnp.maximum(high, part)
    high = jnp.max(high, axis=1, keepdims=True)
    if first:
        new = jnp.broadcast_to(high, (TILE, HD))
    else:
        old = top_ref[span]
        new = jnp.maximum(old, high)
    weights = jnp.concatenate([jnp.exp2(part - new).astype(BF) for part in parts], axis=1)
    total = jnp.dot(weights, value, preferred_element_type=F32)
    if not first:
        shrink = jnp.exp2(old - new)
        total = acc_ref[span] * jnp.concatenate([shrink, shrink], axis=1) + total
    acc_ref[span] = total
    top_ref[span] = new


def attend(scaled_ref, acc_ref, top_ref, block, mask=None, first=False):
    keys, count = block[:, :HD], block.shape[0]
    key = jnp.concatenate([keys, keys], axis=1)
    value = jnp.concatenate([block[:, HD:], jnp.ones((count, HD), BF)], axis=1)
    for number in range(QROWS // TILE):
        one = mask(number) if mask is not None else None
        tile(scaled_ref, acc_ref, top_ref, number * TILE, key, value, one, first)


def own_tokens(query_ref, local_ref, scaled_ref, acc_ref, top_ref):
    for half in range(2):
        for g in range(GROUPS):
            part = query_ref[half * HALF : (half + 1) * HALF, g * HD : (g + 1) * HD].astype(F32) * SCALE
            high = part.astype(BF)
            low = (part - high.astype(F32)).astype(BF)
            start = half * HROWS + g * HALF
            scaled_ref[start : start + HALF, :] = jnp.concatenate([high, low], axis=1)
    token = lax.broadcasted_iota(jnp.int32, (TILE, ROWS), 0) % HALF
    key = lax.broadcasted_iota(jnp.int32, (TILE, ROWS), 1)

    def causal(number):
        return key <= token + (number * TILE // HROWS) * HALF

    attend(scaled_ref, acc_ref, top_ref, local_ref[...], causal, first=True)


NEAR = (0, 4, 2, 6)
FAR = (1, 5, 3, 7)


def visit(place_ref, scaled_ref, acc_ref, top_ref, piece, spots, core, anchor):
    y, z, c = position(place_ref)
    me = place_ref[0]
    count = len(spots) * PASS

    def own(anchored):
        def mask(number):
            width = count + (PASS if anchored else 0)
            lane = lax.broadcasted_iota(jnp.int32, (1, width), 1) // PASS
            seen = jnp.zeros((1, width), jnp.bool_)
            for spot, k in enumerate(spots):
                before = (z // (1 << (k.bit_length() - 1))) % 2 == 1 if k else (core < c)
                seen = seen | ((lane == spot) & before)
            if anchored:
                seen = seen | ((lane == len(spots)) & (me > 0) & (core == 0))
            return seen

        return mask

    def anchor_only(number):
        lane = lax.broadcasted_iota(jnp.int32, (1, count + PASS), 1)
        return (lane < count) | (core == 0)

    for row in range(4):
        whole = anchor and row == 0
        width = count + (PASS if whole else 0)

        @pl.when(row < y)
        def _():
            attend(scaled_ref, acc_ref, top_ref, piece[row, :width], anchor_only if whole else None)

        @pl.when(row == y)
        def _():
            attend(scaled_ref, acc_ref, top_ref, piece[row, :width], own(whole))


def attend_near(
    place_ref, query_hbm, key_hbm, value_hbm, ours_hbm, theirs_hbm, scaled_hbm, acc_hbm, top_hbm,
    query_ref, local_ref, ours_ref, theirs_ref, scaled_ref, acc_ref, top_ref, sems,
):
    copies = fetch(
        [
            (query_hbm, query_ref),
            (key_hbm, local_ref.at[:, :HD]),
            (value_hbm, local_ref.at[:, HD:]),
            (ours_hbm, ours_ref),
            (theirs_hbm, theirs_ref),
        ],
        sems,
    )
    wait(copies[:3])
    own_tokens(query_ref, local_ref, scaled_ref, acc_ref, top_ref)
    c = lax.rem(place_ref[0], 2)
    wait(copies[3:4])
    visit(place_ref, scaled_ref, acc_ref, top_ref, ours_ref, NEAR, c, False)
    wait(copies[4:])
    visit(place_ref, scaled_ref, acc_ref, top_ref, theirs_ref, NEAR, 1 - c, False)
    wait(fetch([(scaled_ref, scaled_hbm), (acc_ref, acc_hbm), (top_ref, top_hbm)], sems))


def attend_far(
    place_ref, scaled_hbm, acc_hbm, top_hbm, ours_hbm, theirs_hbm, weight_hbm, away_hbm, attended_hbm,
    out_ref, attended_ref, weight_ref, ours_ref, theirs_ref, scaled_ref, acc_ref, top_ref, sems,
):
    copies = fetch(
        [
            (scaled_hbm, scaled_ref),
            (acc_hbm, acc_ref),
            (top_hbm, top_ref),
            (ours_hbm, ours_ref),
            (theirs_hbm, theirs_ref),
            (weight_hbm, weight_ref),
        ],
        sems,
    )
    c = lax.rem(place_ref[0], 2)
    wait(copies[:4])
    visit(place_ref, scaled_ref, acc_ref, top_ref, ours_ref, FAR, c, True)
    wait(copies[4:5])
    visit(place_ref, scaled_ref, acc_ref, top_ref, theirs_ref, FAR, 1 - c, True)
    result = (acc_ref[:, :HD] / acc_ref[:, HD:]).astype(BF)
    attended = jnp.concatenate(
        [
            jnp.concatenate(
                [result[half * HROWS + g * HALF : half * HROWS + (g + 1) * HALF] for g in range(GROUPS)], axis=1
            )
            for half in range(2)
        ],
        axis=0,
    )
    attended_ref[...] = attended
    sent = [pltpu.make_async_copy(attended_ref, attended_hbm, sems.at[0])]
    sent[0].start()
    wait(copies[5:])
    project(attended, weight_ref, 1 - lax.rem(place_ref[1], 2), out_ref)
    wait(sent + fetch([(out_ref, away_hbm)], sems.at[1:]))


def project(rows, weight_ref, side, out_ref):
    width = out_ref.shape[2]
    for x in range(4):
        columns = pl.ds(pl.multiple_of((2 * x + side) * width, width), width)
        out_ref[x] = jnp.dot(rows, weight_ref[:, columns], preferred_element_type=F32).astype(BF)


def project_home(place_ref, rows_hbm, weight_hbm, home_hbm, out_ref, rows_ref, weight_ref, sems):
    wait(fetch([(rows_hbm, rows_ref), (weight_hbm, weight_ref)], sems))
    project(rows_ref[...], weight_ref, lax.rem(place_ref[1], 2), out_ref)
    wait(fetch([(out_ref, home_hbm)], sems))


def widen(value_ref, out_ref):
    out_ref[...] = value_ref[...].astype(F32)


def add_up(other_ref, parts_ref, out_ref):
    total = other_ref[...]
    for x in range(4):
        total = total + parts_ref[x].astype(F32)
    out_ref[...] = total.astype(BF)


def shape(*dims, dtype=BF):
    return jax.ShapeDtypeStruct(dims, dtype)


def shards(queries, keys, values, passing_index, out_weight):
    me = lax.axis_index("hst")
    head = lax.axis_index("head")

    def over_z(value, k):
        return lax.ppermute(value, "hst", [(i, i ^ (2 * k)) for i in range(64)])

    def over_core(value):
        return lax.ppermute(value, "hst", [(i, i ^ 1) for i in range(64)])

    def four(value):
        return jnp.broadcast_to(value[None], (4,) + value.shape)

    def over_y(value):
        groups = [[16 * row + i for row in range(4)] for i in range(16)]
        return lax.all_to_all(value, "hst", 0, 0, axis_index_groups=groups)

    place = jnp.stack([me, head]).astype(jnp.int32)

    def call(kernel, out_shape, in_specs, out_specs, *args, scratch=(), limit=int(63.75 * 2**20), flops=2**20):
        return pl.pallas_call(
            kernel,
            out_shape=out_shape,
            in_specs=in_specs,
            out_specs=out_specs,
            scratch_shapes=scratch,
            compiler_params=pltpu.CompilerParams(vmem_limit_bytes=limit),
            cost_estimate=pl.CostEstimate(flops=flops, bytes_accessed=2**16, transcendentals=0),
        )(*args)

    def spread(value, k):
        step = 2 * k
        return value + lax.ppermute(value, "hst", [(i, i + step) for i in range(0, 16, 2 * step)])

    def over_x(value):
        return lax.all_to_all(value, "head", 0, 0, axis_index_groups=[[0, 2, 4, 6], [1, 3, 5, 7]])

    copies = pltpu.SemaphoreType.DMA((6,))
    passed, anchor = call(
        prepare,
        (shape(PASS, 2 * HD), shape(ANCHOR, 2 * HD)),
        [SM] + [HBM] * 3,
        (VM,) * 2,
        place,
        passing_index,
        keys,
        values,
        scratch=[pltpu.VMEM((1, PASS), jnp.int32), pltpu.VMEM((ROWS, 2 * HD), BF), copies],
    )

    mirror, anchor = over_z(passed, 4), spread(anchor, 4)
    mirror, anchor = lax.optimization_barrier((mirror, anchor))
    two = jnp.concatenate([passed, mirror], axis=0)
    pair, anchor = lax.optimization_barrier((over_z(two, 2), spread(anchor, 2)))
    near = jnp.concatenate([two, pair], axis=0)
    far = call(
        pack_far,
        shape(4, 5 * PASS, 2 * HD),
        [HBM] * 2,
        HBM,
        over_z(near, 1),
        spread(anchor, 1),
        scratch=[pltpu.VMEM((5 * PASS, 2 * HD), BF), copies],
        flops=2 * 10**9,
    )

    near_y, far = lax.optimization_barrier((over_y(four(near)), far))
    far_y = over_y(far)
    width = GROUPS * HD
    state = [
        pltpu.VMEM((QROWS, 2 * HD), BF),
        pltpu.VMEM((QROWS, 2 * HD), F32),
        pltpu.VMEM((QROWS, HD), F32),
        copies,
    ]
    scaled, acc, top = call(
        attend_near,
        (shape(QROWS, 2 * HD), shape(QROWS, 2 * HD, dtype=F32), shape(QROWS, HD, dtype=F32)),
        [SM] + [HBM] * 5,
        (HBM,) * 3,
        place,
        queries,
        keys,
        values,
        near_y,
        over_core(near_y),
        scratch=[pltpu.VMEM((ROWS, width), BF), pltpu.VMEM((ROWS, 2 * HD), BF)]
        + [pltpu.VMEM(near_y.shape, BF)] * 2
        + state,
    )
    far_y, acc, top = lax.optimization_barrier((far_y, acc, top))
    away, attended = call(
        attend_far,
        (shape(4, ROWS, width), shape(ROWS, width)),
        [SM] + [HBM] * 6,
        (HBM,) * 2,
        place,
        scaled,
        acc,
        top,
        far_y,
        over_core(far_y),
        out_weight,
        scratch=[pltpu.VMEM((4, ROWS, width), BF), pltpu.VMEM((ROWS, width), BF), pltpu.VMEM(out_weight.shape, BF)]
        + [pltpu.VMEM(far_y.shape, BF)] * 2
        + state,
    )

    def sum_over_x(parts):
        return jnp.sum(over_x(parts).astype(F32), axis=0)

    other = lax.ppermute(sum_over_x(away).astype(BF), "head", [(i, i ^ 1) for i in range(8)])
    home = call(
        project_home,
        shape(4, ROWS, width),
        [SM] + [HBM] * 2,
        HBM,
        place,
        attended,
        out_weight,
        scratch=[
            pltpu.VMEM((4, ROWS, width), BF),
            pltpu.VMEM((ROWS, width), BF),
            pltpu.VMEM(out_weight.shape, BF),
            copies,
        ],
    )
    parts = over_x(home)
    return call(
        add_up,
        shape(ROWS, width),
        [VM] * 2,
        VM,
        call(widen, shape(ROWS, width, dtype=F32), [VM], VM, other, limit=2**24, flops=10**11),
        parts,
        limit=2**24,
    )


def solution(mesh):
    in_specs = (
        P("hst", "head"),
        P("hst", "head"),
        P("hst", "head"),
        P("hst", None),
        P("head", None),
    )
    out_specs = P("hst", "head")
    return jax.shard_map(shards, mesh=mesh, in_specs=in_specs, out_specs=out_specs, check_vma=False)
```

```python
import math

import jax
import jax.numpy as jnp
from jax import lax
from jax.experimental import pallas as pl
from jax.experimental.pallas import tpu as pltpu
from jax.sharding import PartitionSpec as P

HD = 128
PASS = 128
ANCHOR = 128
GROUPS = 4
ROWS = 256
HALF = ROWS // 2
QROWS = ROWS * GROUPS
HROWS = HALF * GROUPS
TILE = 512
SCALE = math.log2(math.e) / math.sqrt(HD)
LOW = -1e30
BF = jnp.bfloat16
F32 = jnp.float32
VM = pl.BlockSpec(memory_space=pltpu.VMEM)
SM = pl.BlockSpec(memory_space=pltpu.SMEM)
HBM = pl.BlockSpec(memory_space=pltpu.HBM)


def dot_nt(a, b):
    return lax.dot_general(a, b, (((1,), (1,)), ((), ())), preferred_element_type=F32)


def fetch(pairs, sems):
    copies = [pltpu.make_async_copy(a, b, sems.at[i]) for i, (a, b) in enumerate(pairs)]
    for copy in copies:
        copy.start()
    return copies


def wait(copies):
    for copy in copies:
        copy.wait()


def prepare(place_ref, index_hbm, key_hbm, value_hbm, passed_ref, anchor_ref, index_ref, both_ref, sems):
    wait(
        fetch(
            [(index_hbm, index_ref), (key_hbm, both_ref.at[:, :HD]), (value_hbm, both_ref.at[:, HD:])],
            sems,
        )
    )
    rows = lax.broadcasted_iota(jnp.int32, (ROWS, PASS), 0)
    pick = jnp.where(rows == index_ref[...], 1.0, 0.0).astype(BF)
    both = both_ref[...]
    passed_ref[...] = lax.dot_general(
        pick, both, (((0,), (0,)), ((), ())), preferred_element_type=F32
    ).astype(BF)
    anchor_ref[...] = jnp.where(place_ref[0] == 0, both[:ANCHOR], jnp.zeros_like(both[:ANCHOR]))


def pack_far(pieces_hbm, anchor_hbm, out_hbm, held_ref, sems):
    size = pieces_hbm.shape[0]
    wait(fetch([(pieces_hbm, held_ref.at[:size]), (anchor_hbm, held_ref.at[size:])], sems))
    wait(fetch([(held_ref, out_hbm.at[y]) for y in range(4)], sems))


def position(place_ref):
    me = place_ref[0]
    return me // 16, lax.rem(me // 2, 8), lax.rem(me, 2)


def tile(scaled_ref, acc_ref, top_ref, start, key, value, mask, first):
    span = slice(start, start + TILE)
    s = dot_nt(scaled_ref[span], key)
    if mask is not None:
        s = jnp.where(mask, s, LOW)
    parts = [s[:, j * HD : (j + 1) * HD] for j in range(s.shape[1] // HD)]
    high = parts[0]
    for part in parts[1:]:
        high = jnp.maximum(high, part)
    high = jnp.max(high, axis=1, keepdims=True)
    if first:
        new = jnp.broadcast_to(high, (TILE, HD))
    else:
        old = top_ref[span]
        new = jnp.maximum(old, high)
    weights = jnp.concatenate([jnp.exp2(part - new).astype(BF) for part in parts], axis=1)
    total = jnp.dot(weights, value, preferred_element_type=F32)
    if not first:
        shrink = jnp.exp2(old - new)
        total = acc_ref[span] * jnp.concatenate([shrink, shrink], axis=1) + total
    acc_ref[span] = total
    top_ref[span] = new


def attend(scaled_ref, acc_ref, top_ref, block, mask=None, first=False):
    keys, count = block[:, :HD], block.shape[0]
    key = jnp.concatenate([keys, keys], axis=1)
    value = jnp.concatenate([block[:, HD:], jnp.ones((count, HD), BF)], axis=1)
    for number in range(QROWS // TILE):
        one = mask(number) if mask is not None else None
        tile(scaled_ref, acc_ref, top_ref, number * TILE, key, value, one, first)


def own_tokens(query_ref, local_ref, scaled_ref, acc_ref, top_ref):
    for half in range(2):
        for g in range(GROUPS):
            part = query_ref[half * HALF : (half + 1) * HALF, g * HD : (g + 1) * HD].astype(F32) * SCALE
            high = part.astype(BF)
            low = (part - high.astype(F32)).astype(BF)
            start = half * HROWS + g * HALF
            scaled_ref[start : start + HALF, :] = jnp.concatenate([high, low], axis=1)
    token = lax.broadcasted_iota(jnp.int32, (TILE, ROWS), 0) % HALF
    key = lax.broadcasted_iota(jnp.int32, (TILE, ROWS), 1)

    def causal(number):
        return key <= token + (number * TILE // HROWS) * HALF

    attend(scaled_ref, acc_ref, top_ref, local_ref[...], causal, first=True)


NEAR = (0, 4, 2, 6)
FAR = (1, 5, 3, 7)


def visit(place_ref, scaled_ref, acc_ref, top_ref, pieces_ref, spots):
    y, z, c = position(place_ref)
    count = len(spots) * PASS
    lane = lax.broadcasted_iota(jnp.int32, (1, count), 1) // PASS

    @pl.loop(0, y + 1)
    def _(row):
        for side in range(2):
            core = c if side == 0 else 1 - c
            seen = jnp.zeros((1, count), jnp.int32)
            for spot, k in enumerate(spots):
                before = lax.rem(z // (1 << (k.bit_length() - 1)), 2) == 1 if k else core < c
                seen = jnp.where(lane == spot, (before | (row < y)).astype(jnp.int32), seen)
            attend(scaled_ref, acc_ref, top_ref, pieces_ref[side, row, :count], lambda number: seen > 0)


def visit_anchor(place_ref, scaled_ref, acc_ref, top_ref, pieces_ref):
    me = place_ref[0]

    @pl.when(me > 0)
    def _():
        attend(scaled_ref, acc_ref, top_ref, pieces_ref[lax.rem(me, 2), 0, 4 * PASS :])


def attend_near(
    place_ref, query_hbm, key_hbm, value_hbm, ours_hbm, theirs_hbm, scaled_hbm, acc_hbm, top_hbm,
    query_ref, local_ref, pieces_ref, scaled_ref, acc_ref, top_ref, sems,
):
    copies = fetch(
        [
            (query_hbm, query_ref),
            (key_hbm, local_ref.at[:, :HD]),
            (value_hbm, local_ref.at[:, HD:]),
            (ours_hbm, pieces_ref.at[0]),
            (theirs_hbm, pieces_ref.at[1]),
        ],
        sems,
    )
    wait(copies[:3])
    own_tokens(query_ref, local_ref, scaled_ref, acc_ref, top_ref)
    wait(copies[3:])
    visit(place_ref, scaled_ref, acc_ref, top_ref, pieces_ref, NEAR)
    wait(fetch([(scaled_ref, scaled_hbm), (acc_ref, acc_hbm), (top_ref, top_hbm)], sems))


def attend_far(
    place_ref, scaled_hbm, acc_hbm, top_hbm, ours_hbm, theirs_hbm, weight_hbm, away_hbm, attended_hbm,
    out_ref, attended_ref, weight_ref, pieces_ref, scaled_ref, acc_ref, top_ref, sems,
):
    copies = fetch(
        [
            (scaled_hbm, scaled_ref),
            (acc_hbm, acc_ref),
            (top_hbm, top_ref),
            (ours_hbm, pieces_ref.at[0]),
            (theirs_hbm, pieces_ref.at[1]),
            (weight_hbm, weight_ref),
        ],
        sems,
    )
    wait(copies[:5])
    visit(place_ref, scaled_ref, acc_ref, top_ref, pieces_ref, FAR)
    visit_anchor(place_ref, scaled_ref, acc_ref, top_ref, pieces_ref)
    result = (acc_ref[:, :HD] / acc_ref[:, HD:]).astype(BF)
    attended = jnp.concatenate(
        [
            jnp.concatenate(
                [result[half * HROWS + g * HALF : half * HROWS + (g + 1) * HALF] for g in range(GROUPS)], axis=1
            )
            for half in range(2)
        ],
        axis=0,
    )
    attended_ref[...] = attended
    sent = [pltpu.make_async_copy(attended_ref, attended_hbm, sems.at[0])]
    sent[0].start()
    wait(copies[5:])
    project(attended, weight_ref, 1 - lax.rem(place_ref[1], 2), out_ref)
    wait(sent + fetch([(out_ref, away_hbm)], sems.at[1:]))


def project(rows, weight_ref, side, out_ref):
    width = out_ref.shape[2]
    for x in range(4):
        columns = pl.ds(pl.multiple_of((2 * x + side) * width, width), width)
        out_ref[x] = jnp.dot(rows, weight_ref[:, columns], preferred_element_type=F32).astype(BF)


def project_home(place_ref, rows_hbm, weight_hbm, home_hbm, out_ref, rows_ref, weight_ref, sems):
    wait(fetch([(rows_hbm, rows_ref), (weight_hbm, weight_ref)], sems))
    project(rows_ref[...], weight_ref, lax.rem(place_ref[1], 2), out_ref)
    wait(fetch([(out_ref, home_hbm)], sems))


def widen(value_ref, out_ref):
    out_ref[...] = value_ref[...].astype(F32)


def add_up(other_ref, parts_ref, out_ref):
    total = other_ref[...]
    for x in range(4):
        total = total + parts_ref[x].astype(F32)
    out_ref[...] = total.astype(BF)


def shape(*dims, dtype=BF):
    return jax.ShapeDtypeStruct(dims, dtype)


def shards(queries, keys, values, passing_index, out_weight):
    me = lax.axis_index("hst")
    head = lax.axis_index("head")

    def over_z(value, k):
        return lax.ppermute(value, "hst", [(i, i ^ (2 * k)) for i in range(64)])

    def over_core(value):
        return lax.ppermute(value, "hst", [(i, i ^ 1) for i in range(64)])

    def four(value):
        return jnp.broadcast_to(value[None], (4,) + value.shape)

    def over_y(value):
        groups = [[16 * row + i for row in range(4)] for i in range(16)]
        return lax.all_to_all(value, "hst", 0, 0, axis_index_groups=groups)

    place = jnp.stack([me, head]).astype(jnp.int32)

    def call(kernel, out_shape, in_specs, out_specs, *args, scratch=(), limit=int(63.75 * 2**20), flops=2**20):
        return pl.pallas_call(
            kernel,
            out_shape=out_shape,
            in_specs=in_specs,
            out_specs=out_specs,
            scratch_shapes=scratch,
            compiler_params=pltpu.CompilerParams(vmem_limit_bytes=limit),
            cost_estimate=pl.CostEstimate(flops=flops, bytes_accessed=2**16, transcendentals=0),
        )(*args)

    def spread(value, k):
        step = 2 * k
        return value + lax.ppermute(value, "hst", [(i, i + step) for i in range(0, 16, 2 * step)])

    def over_x(value):
        return lax.all_to_all(value, "head", 0, 0, axis_index_groups=[[0, 2, 4, 6], [1, 3, 5, 7]])

    copies = pltpu.SemaphoreType.DMA((6,))
    passed, anchor = call(
        prepare,
        (shape(PASS, 2 * HD), shape(ANCHOR, 2 * HD)),
        [SM] + [HBM] * 3,
        (VM,) * 2,
        place,
        passing_index,
        keys,
        values,
        scratch=[pltpu.VMEM((1, PASS), jnp.int32), pltpu.VMEM((ROWS, 2 * HD), BF), copies],
    )

    mirror, anchor = over_z(passed, 4), spread(anchor, 4)
    mirror, anchor = lax.optimization_barrier((mirror, anchor))
    two = jnp.concatenate([passed, mirror], axis=0)
    pair, anchor = lax.optimization_barrier((over_z(two, 2), spread(anchor, 2)))
    near = jnp.concatenate([two, pair], axis=0)
    far = call(
        pack_far,
        shape(4, 5 * PASS, 2 * HD),
        [HBM] * 2,
        HBM,
        over_z(near, 1),
        spread(anchor, 1),
        scratch=[pltpu.VMEM((5 * PASS, 2 * HD), BF), copies],
        flops=2 * 10**9,
    )

    near_y, far = lax.optimization_barrier((over_y(four(near)), far))
    far_y = over_y(far)
    width = GROUPS * HD
    state = [
        pltpu.VMEM((QROWS, 2 * HD), BF),
        pltpu.VMEM((QROWS, 2 * HD), F32),
        pltpu.VMEM((QROWS, HD), F32),
        copies,
    ]
    scaled, acc, top = call(
        attend_near,
        (shape(QROWS, 2 * HD), shape(QROWS, 2 * HD, dtype=F32), shape(QROWS, HD, dtype=F32)),
        [SM] + [HBM] * 5,
        (HBM,) * 3,
        place,
        queries,
        keys,
        values,
        near_y,
        over_core(near_y),
        scratch=[pltpu.VMEM((ROWS, width), BF), pltpu.VMEM((ROWS, 2 * HD), BF)]
        + [pltpu.VMEM((2,) + near_y.shape, BF)]
        + state,
    )
    far_y, acc, top = lax.optimization_barrier((far_y, acc, top))
    away, attended = call(
        attend_far,
        (shape(4, ROWS, width), shape(ROWS, width)),
        [SM] + [HBM] * 6,
        (HBM,) * 2,
        place,
        scaled,
        acc,
        top,
        far_y,
        over_core(far_y),
        out_weight,
        scratch=[pltpu.VMEM((4, ROWS, width), BF), pltpu.VMEM((ROWS, width), BF), pltpu.VMEM(out_weight.shape, BF)]
        + [pltpu.VMEM((2,) + far_y.shape, BF)]
        + state,
    )

    home = call(
        project_home,
        shape(4, ROWS, width),
        [SM] + [HBM] * 2,
        HBM,
        place,
        attended,
        out_weight,
        scratch=[
            pltpu.VMEM((4, ROWS, width), BF),
            pltpu.VMEM((ROWS, width), BF),
            pltpu.VMEM(out_weight.shape, BF),
            copies,
        ],
        flops=10**10,
    )
    away, home = lax.optimization_barrier((over_x(away), home))
    other = jnp.sum(away.astype(F32), axis=0).astype(BF)
    other = lax.ppermute(other, "head", [(i, i ^ 1) for i in range(8)])
    parts = over_x(home)
    return call(
        add_up,
        shape(ROWS, width),
        [VM] * 2,
        VM,
        call(widen, shape(ROWS, width, dtype=F32), [VM], VM, other, limit=2**24, flops=10**11),
        parts,
        limit=2**24,
    )


def solution(mesh):
    in_specs = (
        P("hst", "head"),
        P("hst", "head"),
        P("hst", "head"),
        P("hst", None),
        P("head", None),
    )
    out_specs = P("hst", "head")
    return jax.shard_map(shards, mesh=mesh, in_specs=in_specs, out_specs=out_specs, check_vma=False)
```

```python
import math

import jax
import jax.numpy as jnp
from jax import lax
from jax.experimental import pallas as pl
from jax.experimental.pallas import tpu as pltpu
from jax.sharding import PartitionSpec as P

HD = 128
PASS = 128
ANCHOR = 128
GROUPS = 4
ROWS = 256
HALF = ROWS // 2
QROWS = ROWS * GROUPS
HROWS = HALF * GROUPS
TILE = 512
SCALE = math.log2(math.e) / math.sqrt(HD)
LOW = -1e30
BF = jnp.bfloat16
F32 = jnp.float32
VM = pl.BlockSpec(memory_space=pltpu.VMEM)
SM = pl.BlockSpec(memory_space=pltpu.SMEM)
HBM = pl.BlockSpec(memory_space=pltpu.HBM)


def dot_nt(a, b):
    return lax.dot_general(a, b, (((1,), (1,)), ((), ())), preferred_element_type=F32)


def fetch(pairs, sems):
    copies = [pltpu.make_async_copy(a, b, sems.at[i]) for i, (a, b) in enumerate(pairs)]
    for copy in copies:
        copy.start()
    return copies


def wait(copies):
    for copy in copies:
        copy.wait()


def prepare(index_hbm, key_hbm, value_hbm, passed_ref, anchor_ref, index_ref, both_ref, sems):
    wait(
        fetch(
            [(index_hbm, index_ref), (key_hbm, both_ref.at[:, :HD]), (value_hbm, both_ref.at[:, HD:])],
            sems,
        )
    )
    rows = lax.broadcasted_iota(jnp.int32, (ROWS, PASS), 0)
    pick = jnp.where(rows == index_ref[...], 1.0, 0.0).astype(BF)
    both = both_ref[...]
    passed_ref[...] = lax.dot_general(
        pick, both, (((0,), (0,)), ((), ())), preferred_element_type=F32
    ).astype(BF)
    anchor_ref[...] = both[:ANCHOR]


def pack(*refs):
    *pieces, out_ref = refs
    start = 0
    for piece in pieces:
        size = piece.shape[0]
        if len(out_ref.shape) == 2:
            out_ref[start : start + size] = piece[...]
        else:
            for y in range(out_ref.shape[0]):
                out_ref[y, start : start + size] = piece[...]
        start += size


def position(place_ref):
    me = place_ref[0]
    return me // 16, lax.rem(me // 2, 8), lax.rem(me, 2)


def tile(heads_ref, acc_ref, top_ref, start, key, value, mask, first):
    span = slice(start, start + TILE)
    s = dot_nt(heads_ref[span], key)
    if mask is not None:
        s = jnp.where(mask, s, LOW)
    parts = [s[:, j * HD : (j + 1) * HD] for j in range(s.shape[1] // HD)]
    high = parts[0]
    for part in parts[1:]:
        high = jnp.maximum(high, part)
    high = jnp.max(high, axis=1, keepdims=True)
    if first:
        new = jnp.broadcast_to(high, (TILE, HD))
    else:
        old = top_ref[span]
        new = jnp.maximum(old, high)
    weights = jnp.concatenate([jnp.exp2((part - new) * SCALE).astype(BF) for part in parts], axis=1)
    total = jnp.dot(weights, value, preferred_element_type=F32)
    if not first:
        shrink = jnp.exp2((old - new) * SCALE)
        total = acc_ref[span] * jnp.concatenate([shrink, shrink], axis=1) + total
    acc_ref[span] = total
    top_ref[span] = new


def attend(heads_ref, acc_ref, top_ref, block, mask=None, first=False):
    key, count = block[:, :HD], block.shape[0]
    value = jnp.concatenate([block[:, HD:], jnp.ones((count, HD), BF)], axis=1)
    for number in range(QROWS // TILE):
        one = mask(number) if mask is not None else None
        tile(heads_ref, acc_ref, top_ref, number * TILE, key, value, one, first)


def own_tokens(query_ref, local_ref, heads_ref, acc_ref, top_ref):
    for half in range(2):
        for g in range(GROUPS):
            start = half * HROWS + g * HALF
            heads_ref[start : start + HALF, :] = query_ref[half * HALF : (half + 1) * HALF, g * HD : (g + 1) * HD]
    token = lax.broadcasted_iota(jnp.int32, (TILE, ROWS), 0) % HALF
    key = lax.broadcasted_iota(jnp.int32, (TILE, ROWS), 1)

    def causal(number):
        return key <= token + (number * TILE // HROWS) * HALF

    attend(heads_ref, acc_ref, top_ref, local_ref[...], causal, first=True)


NEAR = (0, 4, 2, 6)
FAR = (1, 5, 3, 7)


def visit(place_ref, heads_ref, acc_ref, top_ref, pieces_ref, spots):
    y, z, c = position(place_ref)
    count = len(spots) * PASS
    lane = lax.broadcasted_iota(jnp.int32, (1, count), 1) // PASS

    @pl.loop(0, y + 1)
    def _(row):
        for side in range(2):
            core = c if side == 0 else 1 - c
            seen = jnp.zeros((1, count), jnp.int32)
            for spot, k in enumerate(spots):
                before = lax.rem(z // (1 << (k.bit_length() - 1)), 2) == 1 if k else core < c
                seen = jnp.where(lane == spot, (before | (row < y)).astype(jnp.int32), seen)
            attend(heads_ref, acc_ref, top_ref, pieces_ref[side, row, :count], lambda number: seen > 0)


def visit_anchor(place_ref, heads_ref, acc_ref, top_ref, pieces_ref):
    me = place_ref[0]

    @pl.when(me > 0)
    def _():
        attend(heads_ref, acc_ref, top_ref, pieces_ref[lax.rem(me, 2), 0, 4 * PASS :])


def attend_own(
    place_ref, query_hbm, key_hbm, value_hbm, heads_hbm, acc_hbm, top_hbm,
    query_ref, local_ref, heads_ref, acc_ref, top_ref, sems,
):
    wait(
        fetch(
            [(query_hbm, query_ref), (key_hbm, local_ref.at[:, :HD]), (value_hbm, local_ref.at[:, HD:])],
            sems,
        )
    )
    own_tokens(query_ref, local_ref, heads_ref, acc_ref, top_ref)
    wait(fetch([(heads_ref, heads_hbm), (acc_ref, acc_hbm), (top_ref, top_hbm)], sems))


def attend_near(
    place_ref, heads_hbm, acc_hbm, top_hbm, two_hbm, two2_hbm, pair_hbm, pair2_hbm, acc_out, top_out,
    pieces_ref, heads_ref, acc_ref, top_ref, sems,
):
    wait(
        fetch(
            [
                (heads_hbm, heads_ref),
                (acc_hbm, acc_ref),
                (top_hbm, top_ref),
                (two_hbm, pieces_ref.at[0, :, : 2 * PASS]),
                (two2_hbm, pieces_ref.at[1, :, : 2 * PASS]),
                (pair_hbm, pieces_ref.at[0, :, 2 * PASS :]),
                (pair2_hbm, pieces_ref.at[1, :, 2 * PASS :]),
            ],
            sems,
        )
    )
    visit(place_ref, heads_ref, acc_ref, top_ref, pieces_ref, NEAR)
    wait(fetch([(acc_ref, acc_out), (top_ref, top_out)], sems))


def attend_far(
    place_ref, heads_hbm, acc_hbm, top_hbm, ours_hbm, theirs_hbm, weight_hbm, away_hbm, attended_hbm,
    out_ref, attended_ref, weight_ref, pieces_ref, heads_ref, acc_ref, top_ref, sems,
):
    copies = fetch(
        [
            (heads_hbm, heads_ref),
            (acc_hbm, acc_ref),
            (top_hbm, top_ref),
            (ours_hbm, pieces_ref.at[0]),
            (theirs_hbm, pieces_ref.at[1]),
        ],
        sems,
    )
    wait(copies)
    weights = fetch([(weight_hbm, weight_ref)], sems.at[5:])
    visit(place_ref, heads_ref, acc_ref, top_ref, pieces_ref, FAR)
    visit_anchor(place_ref, heads_ref, acc_ref, top_ref, pieces_ref)
    result = (acc_ref[:, :HD] / acc_ref[:, HD:]).astype(BF)
    attended = jnp.concatenate(
        [
            jnp.concatenate(
                [result[half * HROWS + g * HALF : half * HROWS + (g + 1) * HALF] for g in range(GROUPS)], axis=1
            )
            for half in range(2)
        ],
        axis=0,
    )
    attended_ref[...] = attended
    sent = [pltpu.make_async_copy(attended_ref, attended_hbm, sems.at[0])]
    sent[0].start()
    wait(weights)
    sent += project(attended, weight_ref, 1 - lax.rem(place_ref[1], 2), out_ref, away_hbm, sems.at[1:])
    wait(sent)


def project(rows, weight_ref, side, out_ref, out_hbm, sems):
    width = out_ref.shape[2]
    sent = []
    for x in range(4):
        columns = pl.ds(pl.multiple_of((2 * x + side) * width, width), width)
        out_ref[x] = jnp.dot(rows, weight_ref[:, columns], preferred_element_type=F32).astype(BF)
        sent += fetch([(out_ref.at[x], out_hbm.at[x])], sems.at[x : x + 1])
    return sent


def project_home(place_ref, rows_hbm, weight_hbm, home_hbm, out_ref, rows_ref, weight_ref, sems):
    wait(fetch([(rows_hbm, rows_ref), (weight_hbm, weight_ref)], sems))
    wait(project(rows_ref[...], weight_ref, lax.rem(place_ref[1], 2), out_ref, home_hbm, sems.at[2:]))


def widen(value_ref, out_ref):
    out_ref[...] = value_ref[...].astype(F32)


def add_up(other_ref, parts_ref, out_ref):
    total = other_ref[...]
    for x in range(4):
        total = total + parts_ref[x].astype(F32)
    out_ref[...] = total.astype(BF)


def shape(*dims, dtype=BF):
    return jax.ShapeDtypeStruct(dims, dtype)


def shards(queries, keys, values, passing_index, out_weight):
    me = lax.axis_index("hst")
    head = lax.axis_index("head")

    def over_z(value, k):
        return lax.ppermute(value, "hst", [(i, i ^ (2 * k)) for i in range(64)])

    def over_core(value):
        return lax.ppermute(value, "hst", [(i, i ^ 1) for i in range(64)])

    def over_y(value):
        groups = [[16 * row + i for row in range(4)] for i in range(16)]
        return lax.all_to_all(value, "hst", 0, 0, axis_index_groups=groups)

    place = jnp.stack([me, head]).astype(jnp.int32)

    def call(kernel, out_shape, in_specs, out_specs, *args, scratch=(), limit=int(63.75 * 2**20), flops=2**20):
        return pl.pallas_call(
            kernel,
            out_shape=out_shape,
            in_specs=in_specs,
            out_specs=out_specs,
            scratch_shapes=scratch,
            compiler_params=pltpu.CompilerParams(vmem_limit_bytes=limit),
            cost_estimate=pl.CostEstimate(flops=flops, bytes_accessed=2**16, transcendentals=0),
        )(*args)

    def spread(value, k):
        step = 2 * k
        sent = lax.ppermute(value, "hst", [(i, i + step) for i in range(0, 16, 2 * step)])
        return jnp.where((me < 16) & (me % (2 * step) == step), sent, value)

    def over_x(value):
        return lax.all_to_all(value, "head", 0, 0, axis_index_groups=[[0, 2, 4, 6], [1, 3, 5, 7]])

    copies = pltpu.SemaphoreType.DMA((7,))
    passed, anchor = call(
        prepare,
        (shape(PASS, 2 * HD), shape(ANCHOR, 2 * HD)),
        [HBM] * 3,
        (VM,) * 2,
        passing_index,
        keys,
        values,
        scratch=[pltpu.VMEM((1, PASS), jnp.int32), pltpu.VMEM((ROWS, 2 * HD), BF), copies],
    )

    def packed(*pieces, rows=(4,), flops=10**10):
        size = sum(piece.shape[0] for piece in pieces)
        return call(
            pack,
            shape(*rows, size, 2 * HD),
            [VM] * len(pieces),
            VM,
            *pieces,
            limit=8 * 2**20,
            flops=flops,
        )

    def joined(*pieces):
        return packed(*pieces, rows=(), flops=2**20)

    width = GROUPS * HD
    state = [
        pltpu.VMEM((QROWS, HD), BF),
        pltpu.VMEM((QROWS, 2 * HD), F32),
        pltpu.VMEM((QROWS, HD), F32),
        copies,
    ]
    sums = (shape(QROWS, 2 * HD, dtype=F32), shape(QROWS, HD, dtype=F32))
    mirror = over_z(passed, 4)
    anchor, queries = lax.optimization_barrier((spread(anchor, 4), queries))
    heads, acc, top = call(
        attend_own,
        (shape(QROWS, HD),) + sums,
        [SM] + [HBM] * 3,
        (HBM,) * 3,
        place,
        queries,
        keys,
        values,
        scratch=[pltpu.VMEM((ROWS, width), BF), pltpu.VMEM((ROWS, 2 * HD), BF)] + state,
        flops=10**10,
    )
    mirror, anchor, heads, acc, top = lax.optimization_barrier((mirror, anchor, heads, acc, top))
    two = joined(passed, mirror)
    two_b = packed(two)
    pair, anchor = lax.optimization_barrier((over_z(two, 2), spread(anchor, 2)))
    near = joined(two, pair)
    pair_b = packed(pair)
    far = packed(over_z(near, 1), spread(anchor, 1))
    two_y, pair_b = lax.optimization_barrier((over_y(two_b), pair_b))
    pair_y, far, two_y2 = lax.optimization_barrier((over_y(pair_b), far, over_core(two_y)))
    far_y = over_y(far)
    acc, top = call(
        attend_near,
        sums,
        [SM] + [HBM] * 7,
        (HBM,) * 2,
        place,
        heads,
        acc,
        top,
        two_y,
        two_y2,
        pair_y,
        over_core(pair_y),
        scratch=[pltpu.VMEM((2, 4, 4 * PASS, 2 * HD), BF)] + state,
    )
    far_y, acc, top = lax.optimization_barrier((far_y, acc, top))
    away, attended = call(
        attend_far,
        (shape(4, ROWS, width), shape(ROWS, width)),
        [SM] + [HBM] * 6,
        (HBM,) * 2,
        place,
        heads,
        acc,
        top,
        far_y,
        over_core(far_y),
        out_weight,
        scratch=[pltpu.VMEM((4, ROWS, width), BF), pltpu.VMEM((ROWS, width), BF), pltpu.VMEM(out_weight.shape, BF)]
        + [pltpu.VMEM((2,) + far_y.shape, BF)]
        + state,
    )

    home = call(
        project_home,
        shape(4, ROWS, width),
        [SM] + [HBM] * 2,
        HBM,
        place,
        attended,
        out_weight,
        scratch=[
            pltpu.VMEM((4, ROWS, width), BF),
            pltpu.VMEM((ROWS, width), BF),
            pltpu.VMEM(out_weight.shape, BF),
            copies,
        ],
        flops=10**10,
    )
    away, home = lax.optimization_barrier((over_x(away), home))
    other = jnp.sum(away.astype(F32), axis=0).astype(BF)
    other = lax.ppermute(other, "head", [(i, i ^ 1) for i in range(8)])
    parts = over_x(home)
    return call(
        add_up,
        shape(ROWS, width),
        [VM] * 2,
        VM,
        call(widen, shape(ROWS, width, dtype=F32), [VM], VM, other, limit=2**24, flops=10**11),
        parts,
        limit=2**24,
    )


def solution(mesh):
    in_specs = (
        P("hst", "head"),
        P("hst", "head"),
        P("hst", "head"),
        P("hst", None),
        P("head", None),
    )
    out_specs = P("hst", "head")
    return jax.shard_map(shards, mesh=mesh, in_specs=in_specs, out_specs=out_specs, check_vma=False)
```

```python
import math

import jax
import jax.numpy as jnp
from jax import lax
from jax.experimental import pallas as pl
from jax.experimental.pallas import tpu as pltpu
from jax.sharding import PartitionSpec as P

HD = 128
PASS = 128
ANCHOR = 128
GROUPS = 4
ROWS = 256
HALF = ROWS // 2
QROWS = ROWS * GROUPS
HROWS = HALF * GROUPS
TILE = 512
SCALE = math.log2(math.e) / math.sqrt(HD)
LOW = -1e30
BF = jnp.bfloat16
F32 = jnp.float32
VM = pl.BlockSpec(memory_space=pltpu.VMEM)
SM = pl.BlockSpec(memory_space=pltpu.SMEM)
HBM = pl.BlockSpec(memory_space=pltpu.HBM)


def dot_nt(a, b):
    return lax.dot_general(a, b, (((1,), (1,)), ((), ())), preferred_element_type=F32)


def fetch(pairs, sems):
    copies = [pltpu.make_async_copy(a, b, sems.at[i]) for i, (a, b) in enumerate(pairs)]
    for copy in copies:
        copy.start()
    return copies


def wait(copies):
    for copy in copies:
        copy.wait()


def prepare(index_hbm, key_hbm, value_hbm, passed_ref, anchor_ref, index_ref, both_ref, sems):
    wait(
        fetch(
            [(index_hbm, index_ref), (key_hbm, both_ref.at[:, :HD]), (value_hbm, both_ref.at[:, HD:])],
            sems,
        )
    )
    rows = lax.broadcasted_iota(jnp.int32, (ROWS, PASS), 0)
    pick = jnp.where(rows == index_ref[...], 1.0, 0.0).astype(BF)
    both = both_ref[...]
    passed_ref[...] = lax.dot_general(
        pick, both, (((0,), (0,)), ((), ())), preferred_element_type=F32
    ).astype(BF)
    anchor_ref[...] = both[:ANCHOR]


def pack(*refs):
    *pieces, out_ref = refs
    start = 0
    for piece in pieces:
        size = piece.shape[0]
        if len(out_ref.shape) == 2:
            out_ref[start : start + size] = piece[...]
        else:
            for y in range(out_ref.shape[0]):
                out_ref[y, start : start + size] = piece[...]
        start += size


def position(place_ref):
    me = place_ref[0]
    return me // 16, lax.rem(me // 2, 8), lax.rem(me, 2)


def tile(heads_ref, acc_ref, top_ref, start, key, value, mask, first):
    span = slice(start, start + TILE)
    s = dot_nt(heads_ref[span], key)
    if mask is not None:
        s = jnp.where(mask, s, LOW)
    parts = [s[:, j * HD : (j + 1) * HD] for j in range(s.shape[1] // HD)]
    high = parts[0]
    for part in parts[1:]:
        high = jnp.maximum(high, part)
    high = jnp.max(high, axis=1, keepdims=True)
    if first:
        new = jnp.broadcast_to(high, (TILE, HD))
    else:
        old = top_ref[span]
        new = jnp.maximum(old, high)
    weights = jnp.concatenate([jnp.exp2((part - new) * SCALE).astype(BF) for part in parts], axis=1)
    total = jnp.dot(weights, value, preferred_element_type=F32)
    if not first:
        shrink = jnp.exp2((old - new) * SCALE)
        total = acc_ref[span] * jnp.concatenate([shrink, shrink], axis=1) + total
    acc_ref[span] = total
    top_ref[span] = new


def attend(heads_ref, acc_ref, top_ref, block, mask=None, first=False):
    key, count = block[:, :HD], block.shape[0]
    value = jnp.concatenate([block[:, HD:], jnp.ones((count, HD), BF)], axis=1)
    for number in range(QROWS // TILE):
        one = mask(number) if mask is not None else None
        tile(heads_ref, acc_ref, top_ref, number * TILE, key, value, one, first)


def own_tokens(query_ref, local_ref, heads_ref, acc_ref, top_ref):
    for half in range(2):
        for g in range(GROUPS):
            start = half * HROWS + g * HALF
            heads_ref[start : start + HALF, :] = query_ref[half * HALF : (half + 1) * HALF, g * HD : (g + 1) * HD]
    token = lax.broadcasted_iota(jnp.int32, (TILE, ROWS), 0) % HALF
    key = lax.broadcasted_iota(jnp.int32, (TILE, ROWS), 1)

    def causal(number):
        return key <= token + (number * TILE // HROWS) * HALF

    attend(heads_ref, acc_ref, top_ref, local_ref[...], causal, first=True)


NEAR = (0, 4, 2, 6)
FAR = (1, 5, 3, 7)


def visit(place_ref, heads_ref, acc_ref, top_ref, pieces_ref, spots):
    y, z, c = position(place_ref)
    count = len(spots) * PASS
    lane = lax.broadcasted_iota(jnp.int32, (1, count), 1) // PASS

    @pl.loop(0, y + 1)
    def _(row):
        for side in range(2):
            core = c if side == 0 else 1 - c
            seen = jnp.zeros((1, count), jnp.int32)
            for spot, k in enumerate(spots):
                before = lax.rem(z // (1 << (k.bit_length() - 1)), 2) == 1 if k else core < c
                seen = jnp.where(lane == spot, (before | (row < y)).astype(jnp.int32), seen)
            attend(heads_ref, acc_ref, top_ref, pieces_ref[side, row, :count], lambda number: seen > 0)


def visit_anchor(place_ref, heads_ref, acc_ref, top_ref, pieces_ref):
    me = place_ref[0]

    @pl.when(me > 0)
    def _():
        attend(heads_ref, acc_ref, top_ref, pieces_ref[lax.rem(me, 2), 0, 4 * PASS :])


def attend_own(
    place_ref, query_hbm, key_hbm, value_hbm, heads_hbm, acc_hbm, top_hbm,
    query_ref, local_ref, heads_ref, acc_ref, top_ref, sems,
):
    wait(
        fetch(
            [(query_hbm, query_ref), (key_hbm, local_ref.at[:, :HD]), (value_hbm, local_ref.at[:, HD:])],
            sems,
        )
    )
    own_tokens(query_ref, local_ref, heads_ref, acc_ref, top_ref)
    wait(fetch([(heads_ref, heads_hbm), (acc_ref, acc_hbm), (top_ref, top_hbm)], sems))


def attend_near(
    place_ref, heads_hbm, acc_hbm, top_hbm, two_hbm, two2_hbm, pair_hbm, pair2_hbm, acc_out, top_out,
    pieces_ref, heads_ref, acc_ref, top_ref, sems,
):
    wait(
        fetch(
            [
                (heads_hbm, heads_ref),
                (acc_hbm, acc_ref),
                (top_hbm, top_ref),
                (two_hbm, pieces_ref.at[0, :, : 2 * PASS]),
                (two2_hbm, pieces_ref.at[1, :, : 2 * PASS]),
                (pair_hbm, pieces_ref.at[0, :, 2 * PASS :]),
                (pair2_hbm, pieces_ref.at[1, :, 2 * PASS :]),
            ],
            sems,
        )
    )
    visit(place_ref, heads_ref, acc_ref, top_ref, pieces_ref, NEAR)
    wait(fetch([(acc_ref, acc_out), (top_ref, top_out)], sems))


def attend_far(
    place_ref, heads_hbm, acc_hbm, top_hbm, ours_hbm, theirs_hbm, weight_hbm, away_hbm, attended_hbm,
    out_ref, attended_ref, weight_ref, pieces_ref, heads_ref, acc_ref, top_ref, sems,
):
    copies = fetch(
        [
            (heads_hbm, heads_ref),
            (acc_hbm, acc_ref),
            (top_hbm, top_ref),
            (ours_hbm, pieces_ref.at[0]),
            (theirs_hbm, pieces_ref.at[1]),
        ],
        sems,
    )
    wait(copies)
    weights = fetch([(weight_hbm, weight_ref)], sems.at[5:])
    visit(place_ref, heads_ref, acc_ref, top_ref, pieces_ref, FAR)
    visit_anchor(place_ref, heads_ref, acc_ref, top_ref, pieces_ref)
    result = (acc_ref[:, :HD] / acc_ref[:, HD:]).astype(BF)
    attended = jnp.concatenate(
        [
            jnp.concatenate(
                [result[half * HROWS + g * HALF : half * HROWS + (g + 1) * HALF] for g in range(GROUPS)], axis=1
            )
            for half in range(2)
        ],
        axis=0,
    )
    attended_ref[...] = attended
    sent = [pltpu.make_async_copy(attended_ref, attended_hbm, sems.at[0])]
    sent[0].start()
    wait(weights)
    sent += project(attended, weight_ref, 1 - lax.rem(place_ref[1], 2), out_ref, away_hbm, sems.at[1:])
    wait(sent)


def project(rows, weight_ref, side, out_ref, out_hbm, sems):
    width = out_ref.shape[2]
    sent = []
    for x in range(4):
        columns = pl.ds(pl.multiple_of((2 * x + side) * width, width), width)
        out_ref[x] = jnp.dot(rows, weight_ref[:, columns], preferred_element_type=F32).astype(BF)
        sent += fetch([(out_ref.at[x], out_hbm.at[x])], sems.at[x : x + 1])
    return sent


def project_home(place_ref, rows_hbm, weight_hbm, home_hbm, out_ref, rows_ref, weight_ref, sems):
    wait(fetch([(rows_hbm, rows_ref), (weight_hbm, weight_ref)], sems))
    wait(project(rows_ref[...], weight_ref, lax.rem(place_ref[1], 2), out_ref, home_hbm, sems.at[2:]))


def sum_parts(parts_ref, out_ref):
    total = parts_ref[0].astype(F32)
    for x in range(1, 4):
        total = total + parts_ref[x].astype(F32)
    out_ref[...] = total.astype(BF)


def widen(value_ref, out_ref):
    out_ref[...] = value_ref[...].astype(F32)


def add_up(other_ref, parts_ref, out_ref):
    total = other_ref[...]
    for x in range(4):
        total = total + parts_ref[x].astype(F32)
    out_ref[...] = total.astype(BF)


def shape(*dims, dtype=BF):
    return jax.ShapeDtypeStruct(dims, dtype)


def shards(queries, keys, values, passing_index, out_weight):
    me = lax.axis_index("hst")
    head = lax.axis_index("head")

    def over_z(value, k):
        return lax.ppermute(value, "hst", [(i, i ^ (2 * k)) for i in range(64)])

    def over_core(value):
        return lax.ppermute(value, "hst", [(i, i ^ 1) for i in range(64)])

    def over_y(value):
        groups = [[16 * row + i for row in range(4)] for i in range(16)]
        return lax.all_to_all(value, "hst", 0, 0, axis_index_groups=groups)

    place = jnp.stack([me, head]).astype(jnp.int32)

    def call(kernel, out_shape, in_specs, out_specs, *args, scratch=(), limit=int(63.75 * 2**20), flops=2**20):
        return pl.pallas_call(
            kernel,
            out_shape=out_shape,
            in_specs=in_specs,
            out_specs=out_specs,
            scratch_shapes=scratch,
            compiler_params=pltpu.CompilerParams(vmem_limit_bytes=limit),
            cost_estimate=pl.CostEstimate(flops=flops, bytes_accessed=2**16, transcendentals=0),
        )(*args)

    def spread(value, k):
        step = 2 * k
        sent = lax.ppermute(value, "hst", [(i, i + step) for i in range(0, 16, 2 * step)])
        return jnp.where((me < 16) & (me % (2 * step) == step), sent, value)

    def over_x(value):
        return lax.all_to_all(value, "head", 0, 0, axis_index_groups=[[0, 2, 4, 6], [1, 3, 5, 7]])

    copies = pltpu.SemaphoreType.DMA((7,))
    three = pltpu.SemaphoreType.DMA((3,))
    passed, anchor = call(
        prepare,
        (shape(PASS, 2 * HD), shape(ANCHOR, 2 * HD)),
        [HBM] * 3,
        (VM,) * 2,
        passing_index,
        keys,
        values,
        scratch=[pltpu.VMEM((1, PASS), jnp.int32), pltpu.VMEM((ROWS, 2 * HD), BF), three],
    )

    def packed(*pieces, rows=(4,), flops=10**10):
        size = sum(piece.shape[0] for piece in pieces)
        return call(
            pack,
            shape(*rows, size, 2 * HD),
            [VM] * len(pieces),
            VM,
            *pieces,
            limit=8 * 2**20,
            flops=flops,
        )

    def joined(*pieces):
        return packed(*pieces, rows=(), flops=2**20)

    width = GROUPS * HD
    state = [
        pltpu.VMEM((QROWS, HD), BF),
        pltpu.VMEM((QROWS, 2 * HD), F32),
        pltpu.VMEM((QROWS, HD), F32),
        copies,
    ]
    sums = (shape(QROWS, 2 * HD, dtype=F32), shape(QROWS, HD, dtype=F32))
    mirror = over_z(passed, 4)
    anchor, queries = lax.optimization_barrier((spread(anchor, 4), queries))
    heads, acc, top = call(
        attend_own,
        (shape(QROWS, HD),) + sums,
        [SM] + [HBM] * 3,
        (HBM,) * 3,
        place,
        queries,
        keys,
        values,
        scratch=[pltpu.VMEM((ROWS, width), BF), pltpu.VMEM((ROWS, 2 * HD), BF)] + state,
        flops=10**10,
    )
    mirror, anchor, heads, acc, top = lax.optimization_barrier((mirror, anchor, heads, acc, top))
    two = joined(passed, mirror)
    two_b = packed(two)
    pair, anchor = lax.optimization_barrier((over_z(two, 2), spread(anchor, 2)))
    near = joined(two, pair)
    pair_b = packed(pair)
    far = packed(over_z(near, 1), spread(anchor, 1))
    two_y, pair_b = lax.optimization_barrier((over_y(two_b), pair_b))
    pair_y, far, two_y2 = lax.optimization_barrier((over_y(pair_b), far, over_core(two_y)))
    far_y = over_y(far)
    acc, top = call(
        attend_near,
        sums,
        [SM] + [HBM] * 7,
        (HBM,) * 2,
        place,
        heads,
        acc,
        top,
        two_y,
        two_y2,
        pair_y,
        over_core(pair_y),
        limit=3 * 2**23,
        scratch=[pltpu.VMEM((2, 4, 4 * PASS, 2 * HD), BF)] + state,
    )
    far_y, acc, top = lax.optimization_barrier((far_y, acc, top))
    away, attended = call(
        attend_far,
        (shape(4, ROWS, width), shape(ROWS, width)),
        [SM] + [HBM] * 6,
        (HBM,) * 2,
        place,
        heads,
        acc,
        top,
        far_y,
        over_core(far_y),
        out_weight,
        scratch=[pltpu.VMEM((4, ROWS, width), BF), pltpu.VMEM((ROWS, width), BF), pltpu.VMEM(out_weight.shape, BF)]
        + [pltpu.VMEM((2,) + far_y.shape, BF)]
        + state,
    )

    home = call(
        project_home,
        shape(4, ROWS, width),
        [SM] + [HBM] * 2,
        HBM,
        place,
        attended,
        out_weight,
        scratch=[
            pltpu.VMEM((4, ROWS, width), BF),
            pltpu.VMEM((ROWS, width), BF),
            pltpu.VMEM(out_weight.shape, BF),
            copies,
        ],
        limit=2**24,
        flops=10**10,
    )
    away, home = lax.optimization_barrier((over_x(away), home))
    other = call(sum_parts, shape(ROWS, width), [VM], VM, away, limit=2**24)
    other = lax.ppermute(other, "head", [(i, i ^ 1) for i in range(8)])
    parts = over_x(home)
    return call(
        add_up,
        shape(ROWS, width),
        [VM] * 2,
        VM,
        call(widen, shape(ROWS, width, dtype=F32), [VM], VM, other, limit=2**24, flops=10**11),
        parts,
        limit=2**24,
    )


def solution(mesh):
    in_specs = (
        P("hst", "head"),
        P("hst", "head"),
        P("hst", "head"),
        P("hst", None),
        P("head", None),
    )
    out_specs = P("hst", "head")
    return jax.shard_map(shards, mesh=mesh, in_specs=in_specs, out_specs=out_specs, check_vma=False)
```

```python
import math

import jax
import jax.numpy as jnp
from jax import lax
from jax.experimental import pallas as pl
from jax.experimental.pallas import tpu as pltpu
from jax.sharding import PartitionSpec as P

HD = 128
PASS = 128
ANCHOR = 128
GROUPS = 4
ROWS = 256
HALF = ROWS // 2
QROWS = ROWS * GROUPS
HROWS = HALF * GROUPS
TILE = 512
SCALE = math.log2(math.e) / math.sqrt(HD)
LOW = -1e30
BF = jnp.bfloat16
F32 = jnp.float32
VM = pl.BlockSpec(memory_space=pltpu.VMEM)
SM = pl.BlockSpec(memory_space=pltpu.SMEM)
HBM = pl.BlockSpec(memory_space=pltpu.HBM)


def dot_nt(a, b):
    return lax.dot_general(a, b, (((1,), (1,)), ((), ())), preferred_element_type=F32)


def fetch(pairs, sems):
    copies = [pltpu.make_async_copy(a, b, sems.at[i]) for i, (a, b) in enumerate(pairs)]
    for copy in copies:
        copy.start()
    return copies


def wait(copies):
    for copy in copies:
        copy.wait()


def prepare(index_hbm, key_hbm, value_hbm, passed_ref, anchor_ref, index_ref, both_ref, sems):
    wait(
        fetch(
            [(index_hbm, index_ref), (key_hbm, both_ref.at[:, :HD]), (value_hbm, both_ref.at[:, HD:])],
            sems,
        )
    )
    rows = lax.broadcasted_iota(jnp.int32, (ROWS, PASS), 0)
    pick = jnp.where(rows == index_ref[...], 1.0, 0.0).astype(BF)
    both = both_ref[...]
    passed_ref[...] = lax.dot_general(
        pick, both, (((0,), (0,)), ((), ())), preferred_element_type=F32
    ).astype(BF)
    anchor_ref[...] = both[:ANCHOR]


def pack(*refs):
    *pieces, out_ref = refs
    start = 0
    for piece in pieces:
        size = piece.shape[0]
        if len(out_ref.shape) == 2:
            out_ref[start : start + size] = piece[...]
        else:
            for y in range(out_ref.shape[0]):
                out_ref[y, start : start + size] = piece[...]
        start += size


def position(place_ref):
    me = place_ref[0]
    return me // 16, lax.rem(me // 2, 8), lax.rem(me, 2)


def tile(heads_ref, acc_ref, top_ref, start, key, value, mask, first):
    span = slice(start, start + TILE)
    s = dot_nt(heads_ref[span], key)
    if mask is not None:
        s = jnp.where(mask, s, LOW)
    parts = [s[:, j * HD : (j + 1) * HD] for j in range(s.shape[1] // HD)]
    high = parts[0]
    for part in parts[1:]:
        high = jnp.maximum(high, part)
    high = jnp.max(high, axis=1, keepdims=True)
    if first:
        new = jnp.broadcast_to(high, (TILE, HD))
    else:
        old = top_ref[span]
        new = jnp.maximum(old, high)
    weights = jnp.concatenate([jnp.exp2((part - new) * SCALE).astype(BF) for part in parts], axis=1)
    total = jnp.dot(weights, value, preferred_element_type=F32)
    if not first:
        shrink = jnp.exp2((old - new) * SCALE)
        total = acc_ref[span] * jnp.concatenate([shrink, shrink], axis=1) + total
    acc_ref[span] = total
    top_ref[span] = new


def attend(heads_ref, acc_ref, top_ref, block, mask=None, first=False):
    key, count = block[:, :HD], block.shape[0]
    value = jnp.concatenate([block[:, HD:], jnp.ones((count, HD), BF)], axis=1)
    for number in range(QROWS // TILE):
        one = mask(number) if mask is not None else None
        tile(heads_ref, acc_ref, top_ref, number * TILE, key, value, one, first)


def own_tokens(query_ref, local_ref, heads_ref, acc_ref, top_ref):
    for half in range(2):
        for g in range(GROUPS):
            start = half * HROWS + g * HALF
            heads_ref[start : start + HALF, :] = query_ref[half * HALF : (half + 1) * HALF, g * HD : (g + 1) * HD]
    token = lax.broadcasted_iota(jnp.int32, (TILE, ROWS), 0) % HALF
    key = lax.broadcasted_iota(jnp.int32, (TILE, ROWS), 1)

    def causal(number):
        return key <= token + (number * TILE // HROWS) * HALF

    attend(heads_ref, acc_ref, top_ref, local_ref[...], causal, first=True)


NEAR = (0, 4, 2, 6)
FAR = (1, 5, 3, 7)


def visit(place_ref, heads_ref, acc_ref, top_ref, piece, spots):
    y, z, c = position(place_ref)
    count = len(spots) * PASS
    lane = lax.broadcasted_iota(jnp.int32, (1, count), 1) // PASS

    @pl.loop(0, y + 1)
    def _(row):
        for side in range(2):
            core = c if side == 0 else 1 - c
            seen = jnp.zeros((1, count), jnp.int32)
            for spot, k in enumerate(spots):
                before = lax.rem(z // (1 << (k.bit_length() - 1)), 2) == 1 if k else core < c
                seen = jnp.where(lane == spot, (before | (row < y)).astype(jnp.int32), seen)
            attend(heads_ref, acc_ref, top_ref, piece(side, row), lambda number: seen > 0)


def visit_anchor(place_ref, heads_ref, acc_ref, top_ref, pieces_ref):
    me = place_ref[0]

    @pl.when(me > 0)
    def _():
        attend(heads_ref, acc_ref, top_ref, pieces_ref[lax.rem(me, 2), 0, 4 * PASS :])


def attend_own(
    place_ref, query_hbm, key_hbm, value_hbm, heads_hbm, acc_hbm, top_hbm,
    query_ref, local_ref, heads_ref, acc_ref, top_ref, sems,
):
    wait(
        fetch(
            [(query_hbm, query_ref), (key_hbm, local_ref.at[:, :HD]), (value_hbm, local_ref.at[:, HD:])],
            sems,
        )
    )
    own_tokens(query_ref, local_ref, heads_ref, acc_ref, top_ref)
    wait(fetch([(heads_ref, heads_hbm), (acc_ref, acc_hbm), (top_ref, top_hbm)], sems))


def attend_near(
    place_ref, heads_ref, acc_in, top_in, two_ref, two2_ref, pair_ref, pair2_ref, acc_ref, top_ref,
):
    acc_ref[...] = acc_in[...]
    top_ref[...] = top_in[...]
    sides = ((two_ref, pair_ref), (two2_ref, pair2_ref))

    def piece(side, row):
        return jnp.concatenate([ref[row] for ref in sides[side]], axis=0)

    visit(place_ref, heads_ref, acc_ref, top_ref, piece, NEAR)


def attend_far(
    place_ref, heads_hbm, acc_hbm, top_hbm, ours_hbm, theirs_hbm, weight_hbm, away_hbm, attended_hbm,
    out_ref, attended_ref, weight_ref, pieces_ref, heads_ref, acc_ref, top_ref, sems,
):
    copies = fetch(
        [
            (heads_hbm, heads_ref),
            (acc_hbm, acc_ref),
            (top_hbm, top_ref),
            (ours_hbm, pieces_ref.at[0]),
            (theirs_hbm, pieces_ref.at[1]),
        ],
        sems,
    )
    wait(copies)
    weights = fetch([(weight_hbm, weight_ref)], sems.at[5:])
    visit(place_ref, heads_ref, acc_ref, top_ref, lambda side, row: pieces_ref[side, row, : 4 * PASS], FAR)
    visit_anchor(place_ref, heads_ref, acc_ref, top_ref, pieces_ref)
    result = (acc_ref[:, :HD] / acc_ref[:, HD:]).astype(BF)
    attended = jnp.concatenate(
        [
            jnp.concatenate(
                [result[half * HROWS + g * HALF : half * HROWS + (g + 1) * HALF] for g in range(GROUPS)], axis=1
            )
            for half in range(2)
        ],
        axis=0,
    )
    attended_ref[...] = attended
    sent = [pltpu.make_async_copy(attended_ref, attended_hbm, sems.at[0])]
    sent[0].start()
    wait(weights)
    sent += project(attended, weight_ref, 1 - lax.rem(place_ref[1], 2), out_ref, away_hbm, sems.at[1:])
    wait(sent)


def project(rows, weight_ref, side, out_ref, out_hbm, sems):
    width = out_ref.shape[2]
    sent = []
    for x in range(4):
        columns = pl.ds(pl.multiple_of((2 * x + side) * width, width), width)
        out_ref[x] = jnp.dot(rows, weight_ref[:, columns], preferred_element_type=F32).astype(BF)
        sent += fetch([(out_ref.at[x], out_hbm.at[x])], sems.at[x : x + 1])
    return sent


def project_home(place_ref, rows_hbm, weight_hbm, home_hbm, out_ref, rows_ref, weight_ref, sems):
    wait(fetch([(rows_hbm, rows_ref), (weight_hbm, weight_ref)], sems))
    wait(project(rows_ref[...], weight_ref, lax.rem(place_ref[1], 2), out_ref, home_hbm, sems.at[2:]))


def sum_parts(parts_ref, out_ref):
    total = parts_ref[0].astype(F32)
    for x in range(1, 4):
        total = total + parts_ref[x].astype(F32)
    out_ref[...] = total.astype(BF)


def widen(value_ref, out_ref):
    out_ref[...] = value_ref[...].astype(F32)


def add_up(other_ref, parts_ref, out_ref):
    total = other_ref[...]
    for x in range(4):
        total = total + parts_ref[x].astype(F32)
    out_ref[...] = total.astype(BF)


def shape(*dims, dtype=BF):
    return jax.ShapeDtypeStruct(dims, dtype)


def shards(queries, keys, values, passing_index, out_weight):
    me = lax.axis_index("hst")
    head = lax.axis_index("head")

    def over_z(value, k):
        return lax.ppermute(value, "hst", [(i, i ^ (2 * k)) for i in range(64)])

    def over_core(value):
        return lax.ppermute(value, "hst", [(i, i ^ 1) for i in range(64)])

    def over_y(value):
        groups = [[16 * row + i for row in range(4)] for i in range(16)]
        return lax.all_to_all(value, "hst", 0, 0, axis_index_groups=groups)

    place = jnp.stack([me, head]).astype(jnp.int32)

    def call(kernel, out_shape, in_specs, out_specs, *args, scratch=(), limit=int(63.75 * 2**20), flops=2**20):
        return pl.pallas_call(
            kernel,
            out_shape=out_shape,
            in_specs=in_specs,
            out_specs=out_specs,
            scratch_shapes=scratch,
            compiler_params=pltpu.CompilerParams(vmem_limit_bytes=limit),
            cost_estimate=pl.CostEstimate(flops=flops, bytes_accessed=2**16, transcendentals=0),
        )(*args)

    def spread(value, k):
        step = 2 * k
        sent = lax.ppermute(value, "hst", [(i, i + step) for i in range(0, 16, 2 * step)])
        return jnp.where((me < 16) & (me % (2 * step) == step), sent, value)

    def over_x(value):
        return lax.all_to_all(value, "head", 0, 0, axis_index_groups=[[0, 2, 4, 6], [1, 3, 5, 7]])

    copies = pltpu.SemaphoreType.DMA((7,))
    three = pltpu.SemaphoreType.DMA((3,))
    passed, anchor = call(
        prepare,
        (shape(PASS, 2 * HD), shape(ANCHOR, 2 * HD)),
        [HBM] * 3,
        (VM,) * 2,
        passing_index,
        keys,
        values,
        scratch=[pltpu.VMEM((1, PASS), jnp.int32), pltpu.VMEM((ROWS, 2 * HD), BF), three],
    )

    def packed(*pieces, rows=(4,), flops=10**10):
        size = sum(piece.shape[0] for piece in pieces)
        return call(
            pack,
            shape(*rows, size, 2 * HD),
            [VM] * len(pieces),
            VM,
            *pieces,
            limit=8 * 2**20,
            flops=flops,
        )

    def joined(*pieces):
        return packed(*pieces, rows=(), flops=2**20)

    width = GROUPS * HD
    state = [
        pltpu.VMEM((QROWS, HD), BF),
        pltpu.VMEM((QROWS, 2 * HD), F32),
        pltpu.VMEM((QROWS, HD), F32),
        copies,
    ]
    sums = (shape(QROWS, 2 * HD, dtype=F32), shape(QROWS, HD, dtype=F32))
    mirror = over_z(passed, 4)
    anchor, queries = lax.optimization_barrier((spread(anchor, 4), queries))
    heads, acc, top = call(
        attend_own,
        (shape(QROWS, HD),) + sums,
        [SM] + [HBM] * 3,
        (HBM,) * 3,
        place,
        queries,
        keys,
        values,
        scratch=[pltpu.VMEM((ROWS, width), BF), pltpu.VMEM((ROWS, 2 * HD), BF)] + state,
        flops=10**10,
    )
    mirror, anchor, heads, acc, top = lax.optimization_barrier((mirror, anchor, heads, acc, top))
    two = joined(passed, mirror)
    two_b = packed(two)
    pair, anchor = lax.optimization_barrier((over_z(two, 2), spread(anchor, 2)))
    near = joined(two, pair)
    pair_b = packed(pair)
    far = packed(over_z(near, 1), spread(anchor, 1))
    two_y, pair_b = lax.optimization_barrier((over_y(two_b), pair_b))
    pair_y, far, two_y2 = lax.optimization_barrier((over_y(pair_b), far, over_core(two_y)))
    far_y = over_y(far)
    acc, top = call(
        attend_near,
        sums,
        [SM] + [VM] * 7,
        (VM,) * 2,
        place,
        heads,
        acc,
        top,
        two_y,
        two_y2,
        pair_y,
        over_core(pair_y),
        limit=3 * 2**23,
    )
    far_y, acc, top = lax.optimization_barrier((far_y, acc, top))
    away, attended = call(
        attend_far,
        (shape(4, ROWS, width), shape(ROWS, width)),
        [SM] + [HBM] * 6,
        (HBM,) * 2,
        place,
        heads,
        acc,
        top,
        far_y,
        over_core(far_y),
        out_weight,
        scratch=[pltpu.VMEM((4, ROWS, width), BF), pltpu.VMEM((ROWS, width), BF), pltpu.VMEM(out_weight.shape, BF)]
        + [pltpu.VMEM((2,) + far_y.shape, BF)]
        + state,
    )

    home = call(
        project_home,
        shape(4, ROWS, width),
        [SM] + [HBM] * 2,
        HBM,
        place,
        attended,
        out_weight,
        scratch=[
            pltpu.VMEM((4, ROWS, width), BF),
            pltpu.VMEM((ROWS, width), BF),
            pltpu.VMEM(out_weight.shape, BF),
            copies,
        ],
        limit=2**24,
        flops=10**10,
    )
    away, home = lax.optimization_barrier((over_x(away), home))
    other = call(sum_parts, shape(ROWS, width), [VM], VM, away, limit=2**24)
    other = lax.ppermute(other, "head", [(i, i ^ 1) for i in range(8)])
    parts = over_x(home)
    return call(
        add_up,
        shape(ROWS, width),
        [VM] * 2,
        VM,
        call(widen, shape(ROWS, width, dtype=F32), [VM], VM, other, limit=2**24, flops=10**11),
        parts,
        limit=2**24,
    )


def solution(mesh):
    in_specs = (
        P("hst", "head"),
        P("hst", "head"),
        P("hst", "head"),
        P("hst", None),
        P("head", None),
    )
    out_specs = P("hst", "head")
    return jax.shard_map(shards, mesh=mesh, in_specs=in_specs, out_specs=out_specs, check_vma=False)
```
